512 devices in a mesh: comp: 64 (over x, z, core), lat: 8 (over y).
Axes of the slice: x: 4, y: 8, z: 8, core: 2. Of those that a mesh axis runs over, the one named last changes fastest.
Arguments:
- spectrum: bfloat16 [1152, 65536], P(None, ('lat', 'comp')), may hold values from 0.049804688 to 2
- sea_cells: int32 [8, 8192], P('lat'), may hold values from 0 to 8191, as said below
- sea_count: int32 [8], P('lat'), may hold values from 4096 to 8192, as said below
- refraction: float32 [8, 8192], P('lat'), may hold values from -0.45 to 0.45
- wind_speed: float32 [8, 8192], P('lat'), may hold values from 0.5 to 5
- growth: float32 [1152], replicated, may hold values from 0.02 to 0.2
- damping: float32 [1152], replicated, may hold values from 0.05 to 0.5
- courant: float32 [32], replicated, may hold values from 0.15 to 0.35
Outputs:
- propagated: float32 [1152, 128, 512], P('comp', 'lat')
The draws below stay inside these ranges and needn't reach their ends.
Inputs may be any that keep to these rules, and one draw needn't show every extreme that they name: `sea_cells`: the 8192 entries of a tile are distinct cells of its 16 x 512 block; the first sea_count of them are its sea points in slot order. `sea_count`: one tile has exactly 8192 sea points.
All inputs are finite; a program needn't handle non-finite values.
Results may differ from the reference program's by a relative error of at most 0.006.
Values may be sent and summed in bfloat16 or wider, within the bound.
A program may use at most 64 MiB of HBM per device.

```python
import math
import jax
import jax.numpy as jnp
from jax import lax

NDIR = 36
NFREQ = 32
NCOMP = 1152
ROWS = 16
LON = 512
PROP_STEPS = 2
TILES = 8
SLOTS = 8192


def draw_sea_cells(key, part):
    key = jax.random.fold_in(key, 11)
    tile_keys = jax.random.split(key, TILES)

    def shuffle(tile_key):
        return jax.random.permutation(tile_key, ROWS * LON)[:SLOTS].astype(jnp.int32)
    return jax.vmap(shuffle)(tile_keys)


def draw_sea_count(key, part):
    key = jax.random.fold_in(key, 23)
    key_counts, key_full = jax.random.split(key)
    counts = jax.random.randint(key_counts, (TILES,), SLOTS // 2, SLOTS + 1)
    full_tile = jax.random.randint(key_full, (), 0, TILES)
    return jnp.where(jnp.arange(TILES, dtype=jnp.int32) == full_tile, SLOTS, counts).astype(jnp.int32)


def level_of(key, extent, cuts, low, top_value):
    gain, own = 1.0, jax.random.fold_in(key, 6)
    for position, parts in cuts:
        draws = jnp.exp(jax.random.uniform(jax.random.fold_in(own, position), (parts,), jnp.float32, low / len(cuts), top_value / len(cuts)))
        gain = gain * jnp.repeat(draws, extent[position] // parts).reshape([-1 if axis == position else 1 for axis in range(len(extent))])
    return gain


def setup_inputs(seed: int = 0) -> dict:
    splits = jax.random.split(jax.random.key(seed), 9)
    return {
        "spectrum": jnp.clip(jnp.exp(math.log(2.0) - 3.6927934 * jax.random.uniform(splits[0], (NCOMP, TILES * SLOTS), jnp.float32) ** level_of(splits[0], (NCOMP, TILES * SLOTS), ((1, 512),), -0.2, 0.2)), 0.049804688, 2.0).astype(jnp.bfloat16),
        "sea_cells": draw_sea_cells(jax.random.fold_in(splits[8], 71), 0),
        "sea_count": draw_sea_count(jax.random.fold_in(splits[8], 71), 0),
        "refraction": jnp.clip(jax.random.uniform(splits[3], (TILES, SLOTS), jnp.float32, -0.45, 0.45) * level_of(splits[3], (TILES, SLOTS), ((0, 8),), -0.4, 0.0), -0.45, 0.45),
        "wind_speed": jnp.clip(jnp.exp(math.log(5.0) - 2.3025851 * jax.random.uniform(splits[4], (TILES, SLOTS), jnp.float32) ** level_of(splits[4], (TILES, SLOTS), ((0, 8),), -0.2, 0.2)), 0.5, 5.0),
        "growth": jnp.clip(jnp.exp(jax.random.uniform(splits[5], (NCOMP,), jnp.float32, math.log(0.02), math.log(0.2))), 0.02, 0.2),
        "damping": jnp.clip(jnp.exp(jax.random.uniform(splits[6], (NCOMP,), jnp.float32, math.log(0.05), math.log(0.5))), 0.05, 0.5),
        "courant": jnp.clip(jax.random.uniform(splits[7], (NFREQ,), jnp.float32, 0.15, 0.35), 0.15, 0.35),
    }


TWO_PI = 2.0 * math.pi


def refract(energy, bend_rate):
    minus_dir = jnp.roll(energy, 1, axis=-2)
    plus_dir = jnp.roll(energy, -1, axis=-2)
    return energy + jnp.maximum(bend_rate, 0.0) * (minus_dir - energy) + jnp.maximum(-bend_rate, 0.0) * (plus_dir - energy)


def quickest_face(upwind, downwind, farther, courant_number):
    magnitude = jnp.abs(courant_number)
    return 0.5 * (upwind + downwind) - 0.5 * magnitude * (downwind - upwind) - (1.0 - courant_number * courant_number) / 6.0 * (downwind - 2.0 * upwind + farther)


def advance(grid_field, sea_mask, speed_x, speed_y):
    height = grid_field.shape[1]
    interior = grid_field[:, 2:height - 2]
    inner_mask = sea_mask[2:height - 2]
    ahead_cell = jnp.roll(interior, -1, axis=2)
    behind = jnp.roll(interior, 1, axis=2)
    beyond = jnp.roll(interior, -2, axis=2)
    face_x = jnp.where(speed_x >= 0.0, quickest_face(interior, ahead_cell, behind, speed_x), quickest_face(ahead_cell, interior, beyond, speed_x))
    open_x = inner_mask * jnp.roll(inner_mask, -1, axis=1)
    flux_x = speed_x * face_x * open_x
    change_x = flux_x - jnp.roll(flux_x, 1, axis=2)
    lower_row = grid_field[:, 1:height - 2]
    upper_row = grid_field[:, 2:height - 1]
    below_row = grid_field[:, 0:height - 3]
    above_row = grid_field[:, 3:height]
    face_y = jnp.where(speed_y >= 0.0, quickest_face(lower_row, upper_row, below_row, speed_y), quickest_face(upper_row, lower_row, above_row, speed_y))
    open_y = sea_mask[1:height - 2] * sea_mask[2:height - 1]
    flux_y = speed_y * face_y * open_y
    change_y = flux_y[:, 1:] - flux_y[:, :-1]
    return (interior - change_x - change_y) * inner_mask


def reference(spectrum, sea_cells, sea_count, refraction, wind_speed, growth, damping, courant):
    blocks = jnp.transpose(spectrum.reshape(NCOMP, TILES, SLOTS), (1, 0, 2))

    def source_tile(inputs):
        tile_spec, bend_rate, wind_here = inputs
        energy = tile_spec.astype(jnp.float32).reshape(NFREQ, NDIR, SLOTS)
        refracted = refract(energy, bend_rate).reshape(NCOMP, SLOTS)
        mean_energy = jnp.sum(refracted, axis=0) / NCOMP
        net_rate = growth[:, None] * wind_here[None, :] - damping[:, None] * (mean_energy / (mean_energy + 1.0))[None, :]
        return (refracted * jnp.exp(net_rate)).astype(jnp.bfloat16)

    sourced = lax.map(source_tile, (blocks, refraction, wind_speed))
    by_freq = jnp.transpose(sourced.reshape(TILES, NFREQ, NDIR, SLOTS), (1, 0, 2, 3))
    live_slot = jnp.arange(SLOTS, dtype=jnp.int32)[None, :] < sea_count[:, None]
    targets = jnp.where(live_slot, sea_cells, ROWS * LON).astype(jnp.int32)

    def place_mask(target):
        return jnp.zeros((ROWS * LON,), jnp.float32).at[target].set(1.0, mode="drop")

    sea_mask = jax.vmap(place_mask)(targets).reshape(TILES * ROWS, LON)
    angles = jnp.arange(NDIR, dtype=jnp.int32).astype(jnp.float32) * (TWO_PI / NDIR)

    def propagate(inputs):
        values, group_speed = inputs

        def place_values(slot_values, target):
            return jnp.zeros((NDIR, ROWS * LON), jnp.float32).at[:, target].set(slot_values.astype(jnp.float32), mode="drop")

        grid_field = jax.vmap(place_values)(values, targets).reshape(TILES, NDIR, ROWS, LON)
        grid_field = jnp.transpose(grid_field, (1, 0, 2, 3)).reshape(NDIR, TILES * ROWS, LON)
        speed_x = (group_speed * jnp.cos(angles))[:, None, None]
        speed_y = (group_speed * jnp.sin(angles))[:, None, None]
        for substep in range(PROP_STEPS):
            padded = jnp.pad(grid_field, ((0, 0), (2, 2), (0, 0)))
            padded_mask = jnp.pad(sea_mask, ((2, 2), (0, 0)))
            grid_field = advance(padded, padded_mask, speed_x, speed_y)
        return grid_field

    result = lax.map(propagate, (by_freq, courant))
    return result.reshape(NCOMP, TILES * ROWS, LON)
```

```python
import math

import jax
import jax.numpy as jnp
import numpy as np
from jax import lax
from jax.experimental import pallas as pl
from jax.experimental.pallas import tpu as pltpu
from jax.sharding import PartitionSpec as P

MESH = pl.DeviceIdType.MESH
NDIR = 36
NCOMP = 1152
ROWS = 16
LON = 512
TILES = 8
SLOTS = 8192
PEERS = 64
NX, NZ, NCORE = 4, 8, 2
GROUP = NX * NCORE
BLOCK = 128
MINE = NCOMP // PEERS
MAIN = 16
EXT = ROWS + 8
CHUNK = 4 * NDIR

f32 = jnp.float32
bf16 = jnp.bfloat16


def direction_table():
    angles = np.arange(NDIR, dtype=np.float32) * np.float32(2.0 * math.pi / NDIR)
    pick = list(range(MAIN)) + [MAIN, MAIN + 1] * 4
    table = np.zeros((2, 2, 24, 128), np.float32)
    for half in range(2):
        rows = angles[half * MINE + np.array(pick)]
        table[half, 0] = np.cos(rows)[:, None]
        table[half, 1] = np.sin(rows)[:, None]
    return table


def face_weights(speed):
    size = jnp.abs(speed)
    third = (1.0 - speed * speed) / 6.0
    near = (0.5 + 0.5 * size + 2.0 * third) * speed
    far = (0.5 - 0.5 * size - third) * speed
    edge = -third * speed
    ahead = speed >= 0.0
    zero = jnp.zeros_like(speed)
    return (
        jnp.where(ahead, edge, zero),
        jnp.where(ahead, near, far),
        jnp.where(ahead, far, near),
        jnp.where(ahead, zero, edge),
    )


def kernel(
    spec_hbm, cells_hbm, count_hbm, refr_hbm, wind_hbm, growth_hbm, damp_hbm, cour_hbm, table_hbm, out_hbm,
    spec_v, cells_v, count_s, refr_v, wind_v, growth_v, damp_v, cour_s, table_v,
    growth_b, damp_b, bent, send, recv, cols, rowid, mask_bf, mask_in,
    mask_x, open_x, open_y, dense_m, dense_x, dense_y,
    field, mid, tail, tail_d, tail_mid, edge_out, edge_in, out_v,
    in_sem, send_sem, recv_sem, own_sem, mask_send, mask_recv, edge_send, edge_recv, out_sem,
):
    me = lax.axis_index("comp")
    lat = lax.axis_index("lat")
    mx, mz, mc = me // (NZ * NCORE), lax.rem(me, NZ * NCORE) // NCORE, lax.rem(me, NCORE)
    mq = mx * NCORE + mc
    upper, lower = lax.rem(lat + 1, TILES), lax.rem(lat + TILES - 1, TILES)

    barrier = pltpu.get_barrier_semaphore()

    def greet(i, carry):
        other = lax.rem(me + i, PEERS)
        pl.semaphore_signal(barrier, inc=1, device_id={"comp": other}, device_id_type=MESH)
        return carry

    lax.fori_loop(1, PEERS, greet, 0)
    for other in (upper, lower):
        pl.semaphore_signal(barrier, inc=1, device_id={"lat": other}, device_id_type=MESH)

    my_slots = pl.ds(pl.multiple_of(me * BLOCK, BLOCK), BLOCK)
    loads = [
        (spec_hbm, spec_v),
        (cells_hbm, cells_v),
        (count_hbm, count_s),
        (refr_hbm.at[:, my_slots], refr_v),
        (wind_hbm.at[:, my_slots], wind_v),
        (growth_hbm, growth_v),
        (damp_hbm, damp_v),
        (cour_hbm, cour_s),
        (table_hbm.at[lax.rem(me, 2)], table_v),
    ]
    copies = [pltpu.make_async_copy(src, dst, in_sem.at[i]) for i, (src, dst) in enumerate(loads)]
    for copy in copies:
        copy.start()
    for copy in copies:
        copy.wait()

    for j in range(NCOMP // 128):
        part = pl.ds(j * 128, 128)
        growth_b[part, :] = jnp.broadcast_to(growth_v[part].reshape(1, 128), (128, 128)).T
        damp_b[part, :] = jnp.broadcast_to(damp_v[part].reshape(1, 128), (128, 128)).T

    bend = refr_v[...]
    bend_up = jnp.broadcast_to(jnp.maximum(bend, 0.0), (CHUNK, BLOCK))
    bend_down = jnp.broadcast_to(jnp.maximum(-bend, 0.0), (CHUNK, BLOCK))
    dir_of = lax.rem(lax.broadcasted_iota(jnp.int32, (CHUNK, BLOCK), 0), NDIR)

    def refract(g, total):
        part = pl.ds(pl.multiple_of(g * CHUNK, CHUNK), CHUNK)
        energy = spec_v[part, :].astype(f32)
        before = jnp.where(dir_of == 0, pltpu.roll(energy, CHUNK - NDIR + 1, 0), pltpu.roll(energy, 1, 0))
        after = jnp.where(dir_of == NDIR - 1, pltpu.roll(energy, NDIR - 1, 0), pltpu.roll(energy, CHUNK - 1, 0))
        moved = energy + bend_up * (before - energy) + bend_down * (after - energy)
        bent[part, :] = moved
        return total + jnp.sum(moved.reshape(CHUNK // 8, 8, BLOCK), axis=0)

    total = lax.fori_loop(0, NCOMP // CHUNK, refract, jnp.zeros((8, BLOCK), f32))
    mean = jnp.sum(total, axis=0, keepdims=True) / NCOMP
    loss = jnp.broadcast_to(mean / (mean + 1.0), (CHUNK, BLOCK))
    wind = jnp.broadcast_to(wind_v[...], (CHUNK, BLOCK))
    send_rows = send.reshape(NCOMP, BLOCK)

    def source(g, carry):
        part = pl.ds(pl.multiple_of(g * CHUNK, CHUNK), CHUNK)
        rate = growth_b[part, :] * wind - damp_b[part, :] * loss
        send_rows[part, :] = (bent[part, :] * jnp.exp(rate)).astype(bf16)
        return carry

    lax.fori_loop(0, NCOMP // CHUNK, source, 0)

    pl.semaphore_wait(barrier, PEERS - 1 + 2)

    def z_of(k):
        steps = NZ // 2 - (k + 1) // 2
        return lax.rem(mz + jnp.where(lax.rem(k, 2) == 1, steps, NZ - steps), NZ)

    def give(k, j):
        q = lax.rem(mq + j, GROUP)
        other = (q // NCORE) * (NZ * NCORE) + z_of(k) * NCORE + lax.rem(q, NCORE)
        pltpu.make_async_remote_copy(
            src_ref=send.at[other],
            dst_ref=recv.at[mz * GROUP + mq],
            send_sem=send_sem,
            recv_sem=recv_sem.at[mz],
            device_id={"comp": other},
            device_id_type=MESH,
        ).start()

    def give_group(k, carry):
        lax.fori_loop(0, GROUP, lambda j, c: (give(k, j), c)[1], 0)
        return carry

    lax.fori_loop(0, NZ - 1, give_group, 0)
    lax.fori_loop(1, GROUP, lambda j, c: (give(NZ - 1, j), c)[1], 0)
    own = pltpu.make_async_copy(send.at[me], recv.at[mz * GROUP + mq], own_sem)
    own.start()

    live_count = count_s[0]
    lane = lax.broadcasted_iota(jnp.int32, (1, BLOCK), 1)
    col_of = lax.broadcasted_iota(jnp.int16, (LON, BLOCK), 0)
    row_of = lax.broadcasted_iota(jnp.int16, (ROWS, GROUP * BLOCK), 0)

    def factors(z, total):
        for q in range(GROUP):
            first = ((q // NCORE) * (NZ * NCORE) + z * NCORE + q % NCORE) * BLOCK
            cell = cells_v[:, pl.ds(pl.multiple_of(first, BLOCK), BLOCK)]
            col = jnp.broadcast_to(lax.bitwise_and(cell, LON - 1), (LON, BLOCK)).astype(jnp.int16)
            cols[z, :, q * BLOCK : (q + 1) * BLOCK] = jnp.where(col_of == col, bf16(1), bf16(0))
            row = jnp.where(lane + first < live_count, lax.shift_right_logical(cell, 9), ROWS)
            rowid[z, :, q * BLOCK : (q + 1) * BLOCK] = jnp.broadcast_to(row, (ROWS, BLOCK)).astype(jnp.int16)
        hot = jnp.where(rowid[z] == row_of, bf16(1), bf16(0))
        return total + lax.dot_general(hot, cols[z], (((1,), (1,)), ((), ())), preferred_element_type=f32)

    mask = lax.fori_loop(0, NZ, factors, jnp.zeros((ROWS, LON), f32))
    mask_bf[...] = mask.astype(bf16)
    mask_copies = []
    for i, other in enumerate((upper, lower)):
        copy = pltpu.make_async_remote_copy(
            src_ref=mask_bf,
            dst_ref=mask_in.at[i],
            send_sem=mask_send.at[i],
            recv_sem=mask_recv.at[i],
            device_id={"lat": other},
            device_id_type=MESH,
        )
        copy.start()
        mask_copies.append(copy)

    field[...] = jnp.zeros_like(field)
    tail[...] = jnp.zeros_like(tail)
    speed = cour_s[me // 2]
    wx = face_weights(speed * table_v[0])
    wy = face_weights(speed * table_v[1])

    def wide(w):
        return jnp.concatenate([w[:MAIN]] * (LON // 128), axis=1)

    main_x, main_y = [wide(w) for w in wx], [wide(w) for w in wy]
    tail_x, tail_y = [w[MAIN:][None] for w in wx], [w[MAIN:][None] for w in wy]

    for copy in mask_copies:
        copy.wait()
    has_lower = jnp.where(lat > 0, 1.0, 0.0)
    has_upper = jnp.where(lat < TILES - 1, 1.0, 0.0)
    below = mask_in[0].astype(f32)[ROWS - 4 :] * has_lower
    above = mask_in[1].astype(f32)[:4] * has_upper
    full = jnp.concatenate([below, mask, above], axis=0)
    mask_x[...] = full
    open_x[...] = full * pltpu.roll(full, LON - 1, 1)
    open_y[...] = full * pltpu.roll(full, EXT - 1, 0)
    for wide_m, dense in ((mask_x, dense_m), (open_x, dense_x), (open_y, dense_y)):
        for t in range(EXT // 8):
            for b in range(LON // 128):
                piece = wide_m[t * 8 : (t + 1) * 8, b * 128 : (b + 1) * 128]
                for p in range(2):
                    dense[pl.ds(t * 64 + b * 2 + p, 8, stride=8), :] = piece

    recv_rows = recv.reshape(PEERS * MINE, BLOCK)

    def place(z):
        ids = rowid[z]
        main, rest = [], []
        for q in range(GROUP):
            first = (z * GROUP + q) * MINE
            main.append(recv_rows[pl.ds(first, MAIN), :])
            rest.append(recv_rows[pl.ds(first + MAIN, 2), :])
        main = jnp.concatenate(main, axis=1)
        rest = jnp.concatenate(rest, axis=1)
        parts = [jnp.where(ids == r, main, bf16(0)) for r in range(ROWS)]
        for p in range(2):
            line = jnp.broadcast_to(rest[p : p + 1], (ROWS, GROUP * BLOCK))
            parts.append(jnp.where(ids == row_of, line, bf16(0)))
        left = jnp.concatenate(parts, axis=0)
        found = lax.dot_general(left, cols[z], (((1,), (1,)), ((), ())), preferred_element_type=f32)
        field[4 * MAIN : (4 + ROWS) * MAIN, :] += found[: ROWS * MAIN]
        tail[...] += found[ROWS * MAIN :]

    def arrive(z, count):
        block = recv.at[pl.ds(z * GROUP, count)]
        pltpu.make_async_copy(block, block, recv_sem.at[z]).wait()

    def place_group(k, carry):
        z = z_of(k)
        arrive(z, GROUP)
        place(z)
        return carry

    lax.fori_loop(0, NZ - 1, place_group, 0)
    own.wait()
    arrive(mz, GROUP - 1)
    place(mz)

    blank = jnp.zeros((8, LON), f32)
    for i, r in enumerate((ROWS - 4, 0)):
        edge_out[i, : 4 * MAIN, :] = field[(4 + r) * MAIN : (8 + r) * MAIN, :].astype(bf16)
        edge_out[i, 4 * MAIN :, :] = jnp.concatenate(
            [tail[r : r + 4, :], tail[ROWS + r : ROWS + r + 4, :], blank], axis=0
        ).astype(bf16)
    edge_copies = []
    for i, other in enumerate((upper, lower)):
        copy = pltpu.make_async_remote_copy(
            src_ref=edge_out.at[i],
            dst_ref=edge_in.at[i],
            send_sem=edge_send.at[i],
            recv_sem=edge_recv.at[i],
            device_id={"lat": other},
            device_id_type=MESH,
        )
        copy.start()
        edge_copies.append(copy)

    for p in range(2):
        for b in range(LON // 128):
            for t in range(2):
                tail_d[pl.ds(32 + t * 64 + b * 2 + p, 8, stride=8), :] = tail[
                    p * ROWS + t * 8 : p * ROWS + t * 8 + 8, b * 128 : (b + 1) * 128
                ]

    def advance(src, first, last, store):
        def line(ref, e):
            return ref[pl.ds(e, 1), :]

        def rows(e):
            return src[pl.ds(pl.multiple_of(e * MAIN, MAIN), MAIN), :]

        def flux_y(e):
            a, b, c, d = main_y
            return (a * rows(e - 1) + b * rows(e) + c * rows(e + 1) + d * rows(e + 2)) * line(open_y, e)

        def step(e, south):
            here = rows(e)
            a, b, c, d = main_x
            east = (
                a * pltpu.roll(here, 1, 1)
                + b * here
                + c * pltpu.roll(here, LON - 1, 1)
                + d * pltpu.roll(here, LON - 2, 1)
            ) * line(open_x, e)
            north = flux_y(e)
            store(e, (here - (east - pltpu.roll(east, 1, 1)) - (north - south)) * line(mask_x, e))
            return north

        lax.fori_loop(first, last, step, flux_y(first - 1))

    def keep(e, new):
        mid[pl.ds(pl.multiple_of(e * MAIN, MAIN), MAIN), :] = new

    def finish(e, new):
        for b in range(LON // 128):
            for h in range(MAIN // 8):
                out_v[b, pl.ds(h * 8 * ROWS + e - 4, 8, stride=ROWS), :] = new[h * 8 : h * 8 + 8, b * 128 : (b + 1) * 128]

    advance(field, 6, 18, keep)
    advance(mid, 8, 16, finish)

    for copy in edge_copies:
        copy.wait()
    for i, (e, there) in enumerate(((0, has_lower), (EXT - 4, has_upper))):
        field[e * MAIN : (e + 4) * MAIN, :] = edge_in[i, : 4 * MAIN, :].astype(f32) * there
        ghost = edge_in[i, 4 * MAIN :, :].astype(f32) * there
        for p in range(2):
            for b in range(LON // 128):
                tail_d[pl.ds(e * 8 + b * 2 + p, 4, stride=8), :] = ghost[p * 4 : p * 4 + 4, b * 128 : (b + 1) * 128]

    advance(field, 2, 6, keep)
    advance(field, 18, 22, keep)
    advance(mid, 4, 8, finish)
    advance(mid, 16, 20, finish)

    lane3 = lax.broadcasted_iota(jnp.int32, (1, 8, 128), 2)

    def west_of(x):
        turned = pltpu.roll(x, 1, 2)
        return jnp.where(lane3 == 0, pltpu.roll(turned, 2, 1), turned)

    def east_of(x, n):
        turned = pltpu.roll(x, 128 - n, 2)
        return jnp.where(lane3 >= 128 - n, pltpu.roll(turned, 6, 1), turned)

    def advance_tail(full, first):
        count = full.shape[0] - 4
        here = full[2 : count + 2]
        shaped = lambda ref, start, n: ref[start * 8 : (start + n) * 8, :].reshape(n, 8, 128)
        a, b, c, d = tail_x
        east = (a * west_of(here) + b * here + c * east_of(here, 1) + d * east_of(here, 2)) * shaped(
            dense_x, first + 2, count
        )
        a, b, c, d = tail_y
        north = (
            a * full[0 : count + 1] + b * full[1 : count + 2] + c * full[2 : count + 3] + d * full[3 : count + 4]
        ) * shaped(dense_y, first + 1, count + 1)
        return (here - (east - west_of(east)) - (north[1:] - north[:-1])) * shaped(dense_m, first + 2, count)

    ext = tail_d[...].reshape(EXT, 8, 128)
    done = advance_tail(advance_tail(ext, 0), 2)
    tail_mid[...] = done.reshape(ROWS * 8, 128)
    for p in range(2):
        for b in range(LON // 128):
            out_v[b, (MAIN + p) * ROWS : (MAIN + p + 1) * ROWS, :] = tail_mid[pl.ds(b * 2 + p, ROWS, stride=8), :]

    outs = [
        pltpu.make_async_copy(out_v.at[b], out_hbm.at[:, pl.ds(b * 128, 128)], out_sem.at[b]) for b in range(LON // 128)
    ]
    for copy in outs:
        copy.start()
    sent = send.at[pl.ds(0, PEERS - 1)]
    pltpu.make_async_copy(sent, sent, send_sem).wait()
    for copy in outs:
        copy.wait()


def body(spectrum, sea_cells, sea_count, refraction, wind_speed, growth, damping, courant):
    vmem, smem, dma = pltpu.VMEM, pltpu.SMEM, pltpu.SemaphoreType.DMA
    table = jnp.asarray(direction_table())
    block = (PEERS, MINE // 2, 2, BLOCK)
    scratch = [
        vmem((NCOMP, BLOCK), bf16),
        vmem((1, SLOTS), jnp.int32),
        smem((1,), jnp.int32),
        vmem((1, BLOCK), f32),
        vmem((1, BLOCK), f32),
        vmem((NCOMP,), f32),
        vmem((NCOMP,), f32),
        smem((32,), f32),
        vmem((2, 24, 128), f32),
        vmem((NCOMP, BLOCK), f32),
        vmem((NCOMP, BLOCK), f32),
        vmem((NCOMP, BLOCK), f32),
        vmem(block, bf16),
        vmem(block, bf16),
        vmem((NZ, LON, GROUP * BLOCK), bf16),
        vmem((NZ, ROWS, GROUP * BLOCK), jnp.int16),
        vmem((ROWS, LON), bf16),
        vmem((2, ROWS, LON), bf16),
        vmem((EXT, LON), f32),
        vmem((EXT, LON), f32),
        vmem((EXT, LON), f32),
        vmem((EXT * 8, 128), f32),
        vmem((EXT * 8, 128), f32),
        vmem((EXT * 8, 128), f32),
        vmem((EXT * MAIN, LON), f32),
        vmem((EXT * MAIN, LON), f32),
        vmem((2 * ROWS, LON), f32),
        vmem((EXT * 8, 128), f32),
        vmem((ROWS * 8, 128), f32),
        vmem((2, 4 * MAIN + 16, LON), bf16),
        vmem((2, 4 * MAIN + 16, LON), bf16),
        vmem((LON // 128, MINE * ROWS, 128), f32),
        dma((9,)),
        dma,
        dma((NZ,)),
        dma,
        dma((2,)),
        dma((2,)),
        dma((2,)),
        dma((2,)),
        dma((LON // 128,)),
    ]
    out = pl.pallas_call(
        kernel,
        out_shape=jax.ShapeDtypeStruct((MINE * ROWS, LON), f32),
        in_specs=[pl.BlockSpec(memory_space=pl.ANY)] * 9,
        out_specs=pl.BlockSpec(memory_space=pl.ANY),
        scratch_shapes=scratch,
        compiler_params=pltpu.CompilerParams(collective_id=0, has_side_effects=True, vmem_limit_bytes=64 << 20),
        name="wave_step",
    )(spectrum, sea_cells, sea_count, refraction, wind_speed, growth, damping, courant, table)
    return out.reshape(MINE, ROWS, LON)


def solution(mesh):
    return jax.shard_map(
        body,
        mesh=mesh,
        in_specs=(
            P(None, ("lat", "comp")),
            P("lat", None),
            P("lat"),
            P("lat", None),
            P("lat", None),
            P(),
            P(),
            P(),
        ),
        out_specs=P("comp", "lat", None),
        check_vma=False,
    )
```

```python
import math

import jax
import jax.numpy as jnp
import numpy as np
from jax import lax
from jax.experimental import pallas as pl
from jax.experimental.pallas import tpu as pltpu
from jax.sharding import PartitionSpec as P

MESH = pl.DeviceIdType.MESH
NDIR = 36
NCOMP = 1152
ROWS = 16
LON = 512
HALF = LON // 2
TILES = 8
SLOTS = 8192
PEERS = 64
NX, NZ, NCORE = 4, 8, 2
GROUP = NX * NCORE
BLOCK = 128
MINE = NCOMP // PEERS
MAIN = 16
EXT = ROWS + 8
CHUNK = 4 * NDIR

f32 = jnp.float32
bf16 = jnp.bfloat16


FIRST_INNER = ((range(6, 14),), (range(10, 18),))
FIRST_OUTER = ((range(2, 6), range(18, 22)),)
SECOND_INNER = ((range(8, 16),),)
SECOND_OUTER = ((range(4, 8), range(16, 20)),)
GROUPS = FIRST_INNER + FIRST_OUTER + SECOND_INNER + SECOND_OUTER


def direction_table():
    angles = np.arange(NDIR, dtype=np.float32) * np.float32(2.0 * math.pi / NDIR)
    pick = list(range(MAIN)) + [MAIN, MAIN + 1] * 4
    table = np.zeros((2, 2, 32, 128), np.float32)
    for half in range(2):
        rows = angles[half * MINE + np.array(pick)]
        across = np.tile(angles[half * MINE : half * MINE + MAIN], 128 // MAIN)
        for i, wave in enumerate((np.cos, np.sin)):
            table[half, i, :24] = wave(rows)[:, None]
            table[half, i, 24:] = wave(across)[None, :]
    return table


def face_weights(speed):
    size = jnp.abs(speed)
    third = (1.0 - speed * speed) / 6.0
    near = (0.5 + 0.5 * size + 2.0 * third) * speed
    far = (0.5 - 0.5 * size - third) * speed
    ahead = speed >= 0.0
    return ahead, -third * speed, jnp.where(ahead, near, far), jnp.where(ahead, far, near)


def kernel(
    spec_hbm, cells_hbm, count_s, refr_hbm, wind_hbm, growth_hbm, damp_hbm, cour_hbm, table_hbm, out,
    spec_v, cells_v, refr_v, wind_v, growth_v, damp_v, cour_s, table_v,
    growth_b, damp_b, bent, send, recv, cols, rowid, mask_bf, mask_in,
    mask_x, open_x, open_y, turned_open, dense_m, dense_x, dense_y,
    field, mid, tail, tail_d, tail_mid, tail_done, edge_out, edge_in, tail_out, tail_in, out_v,
    in_sem, send_sem, recv_sem, own_sem, mask_send, mask_recv, edge_send, edge_recv,
):
    me = lax.axis_index("comp")
    lat = lax.axis_index("lat")
    mx, mz, mc = me // (NZ * NCORE), lax.rem(me, NZ * NCORE) // NCORE, lax.rem(me, NCORE)
    mq = mx * NCORE + mc
    upper, lower = lax.rem(lat + 1, TILES), lax.rem(lat + TILES - 1, TILES)

    barrier = pltpu.get_barrier_semaphore()

    def z_of(k):
        steps = jnp.where(k == 0, NZ // 2, jnp.where(k == 1, 0, NZ // 2 - k // 2))
        return lax.rem(mz + jnp.where(lax.rem(k, 2) == 0, steps, NZ - steps), NZ)

    def device_of(k, j):
        q = lax.rem(mq + j, GROUP)
        return (q // NCORE) * (NZ * NCORE) + z_of(k) * NCORE + lax.rem(q, NCORE)

    def for_peers(act):
        def group(k, carry):
            return lax.fori_loop(jnp.where(k == 1, 1, 0), GROUP, lambda j, c: (act(device_of(k, j)), c)[1], carry)

        lax.fori_loop(0, NZ, group, 0)

    def greet(other):
        pl.semaphore_signal(barrier, inc=1, device_id={"comp": other}, device_id_type=MESH)

    for_peers(greet)
    for other in (upper, lower):
        pl.semaphore_signal(barrier, inc=1, device_id={"lat": other}, device_id_type=MESH)

    my_slots = pl.ds(pl.multiple_of(me * BLOCK, BLOCK), BLOCK)
    loads = [
        (spec_hbm, spec_v),
        (cells_hbm, cells_v),
        (refr_hbm.at[:, my_slots], refr_v),
        (wind_hbm.at[:, my_slots], wind_v),
        (growth_hbm, growth_v),
        (damp_hbm, damp_v),
        (cour_hbm, cour_s),
        (table_hbm.at[lax.rem(me, 2)], table_v),
    ]
    copies = [pltpu.make_async_copy(src, dst, in_sem.at[i]) for i, (src, dst) in enumerate(loads)]
    for copy in copies:
        copy.start()
    for copy in copies:
        copy.wait()

    for j in range(NCOMP // 128):
        part = pl.ds(j * 128, 128)
        growth_b[part, :] = jnp.broadcast_to(growth_v[part].reshape(1, 128), (128, 128)).T
        damp_b[part, :] = jnp.broadcast_to(damp_v[part].reshape(1, 128), (128, 128)).T

    bend = refr_v[...]
    bend_up = jnp.broadcast_to(jnp.maximum(bend, 0.0), (CHUNK, BLOCK))
    bend_down = jnp.broadcast_to(jnp.maximum(-bend, 0.0), (CHUNK, BLOCK))
    dir_of = lax.rem(lax.broadcasted_iota(jnp.int32, (CHUNK, BLOCK), 0), NDIR)

    def refract(g, total):
        part = pl.ds(pl.multiple_of(g * CHUNK, CHUNK), CHUNK)
        energy = spec_v[part, :].astype(f32)
        before = jnp.where(dir_of == 0, pltpu.roll(energy, CHUNK - NDIR + 1, 0), pltpu.roll(energy, 1, 0))
        after = jnp.where(dir_of == NDIR - 1, pltpu.roll(energy, NDIR - 1, 0), pltpu.roll(energy, CHUNK - 1, 0))
        moved = energy + bend_up * (before - energy) + bend_down * (after - energy)
        bent[part, :] = moved
        return total + jnp.sum(moved.reshape(CHUNK // 8, 8, BLOCK), axis=0)

    total = lax.fori_loop(0, NCOMP // CHUNK, refract, jnp.zeros((8, BLOCK), f32))
    mean = jnp.sum(total, axis=0, keepdims=True) / NCOMP
    loss = jnp.broadcast_to(mean / (mean + 1.0), (CHUNK, BLOCK))
    wind = jnp.broadcast_to(wind_v[...], (CHUNK, BLOCK))
    send_rows = send.reshape(NCOMP, BLOCK)

    def source(g, carry):
        part = pl.ds(pl.multiple_of(g * CHUNK, CHUNK), CHUNK)
        rate = growth_b[part, :] * wind - damp_b[part, :] * loss
        send_rows[part, :] = (bent[part, :] * jnp.exp(rate)).astype(bf16)
        return carry

    lax.fori_loop(0, NCOMP // CHUNK, source, 0)

    pl.semaphore_wait(barrier, PEERS - 1 + 2)

    def give(other):
        pltpu.make_async_remote_copy(
            src_ref=send.at[other],
            dst_ref=recv.at[mz * GROUP + mq],
            send_sem=send_sem,
            recv_sem=recv_sem.at[mz],
            device_id={"comp": other},
            device_id_type=MESH,
        ).start()

    for_peers(give)
    own = pltpu.make_async_copy(send.at[me], recv.at[mz * GROUP + mq], own_sem)
    own.start()

    live_count = count_s[0]
    lane = lax.broadcasted_iota(jnp.int32, (1, BLOCK), 1)
    col_of = lax.broadcasted_iota(jnp.int16, (HALF, BLOCK), 0)
    row_of = 2 * lax.broadcasted_iota(jnp.int16, (ROWS, GROUP * BLOCK), 0)

    def factors(z, total):
        for q in range(GROUP):
            first = ((q // NCORE) * (NZ * NCORE) + z * NCORE + q % NCORE) * BLOCK
            cell = cells_v[:, pl.ds(pl.multiple_of(first, BLOCK), BLOCK)]
            col = jnp.broadcast_to(lax.bitwise_and(cell, HALF - 1), (HALF, BLOCK)).astype(jnp.int16)
            cols[z, :, q * BLOCK : (q + 1) * BLOCK] = jnp.where(col_of == col, bf16(1), bf16(0))
            row = jnp.where(lane + first < live_count, lax.shift_right_logical(cell, 8), 2 * ROWS)
            rowid[z, :, q * BLOCK : (q + 1) * BLOCK] = jnp.broadcast_to(row, (ROWS, BLOCK)).astype(jnp.int16)
        ids = rowid[z]
        hot = jnp.concatenate([jnp.where(ids == row_of + half, bf16(1), bf16(0)) for half in range(2)], axis=0)
        return total + lax.dot_general(hot, cols[z], (((1,), (1,)), ((), ())), preferred_element_type=f32)

    mask = lax.fori_loop(0, NZ, factors, jnp.zeros((2 * ROWS, HALF), f32))
    mask = jnp.concatenate([mask[:ROWS], mask[ROWS:]], axis=1)
    mask_bf[...] = mask.astype(bf16)
    mask_copies = []
    for i, other in enumerate((upper, lower)):
        copy = pltpu.make_async_remote_copy(
            src_ref=mask_bf,
            dst_ref=mask_in.at[i],
            send_sem=mask_send.at[i],
            recv_sem=mask_recv.at[i],
            device_id={"lat": other},
            device_id_type=MESH,
        )
        copy.start()
        mask_copies.append(copy)

    field[...] = jnp.zeros_like(field)
    tail[...] = jnp.zeros_like(tail)
    tail_d[...] = jnp.zeros_like(tail_d)
    speed = cour_s[me // 2]
    wx = face_weights(speed * table_v[0])
    wy = face_weights(speed * table_v[1])

    def wide(x, first, count):
        return jnp.concatenate([x[first : first + count]] * (LON // 128), axis=1)

    main_y = [wide(w, 0, MAIN) for w in wy]
    turned_x = [w[24:][None] for w in wx]
    tail_x, tail_y = [[x[MAIN:24][None] for x in w] for w in (wx, wy)]

    for copy in mask_copies:
        copy.wait()
    has_lower = jnp.where(lat > 0, 1.0, 0.0)
    has_upper = jnp.where(lat < TILES - 1, 1.0, 0.0)
    below = mask_in[0].astype(f32)[ROWS - 4 :] * has_lower
    above = mask_in[1].astype(f32)[:4] * has_upper
    full = jnp.concatenate([below, mask, above], axis=0)
    mask_x[...] = full
    open_x[...] = full * pltpu.roll(full, LON - 1, 1)
    open_y[...] = full * pltpu.roll(full, EXT - 1, 0)
    for wide_m, dense in ((mask_x, dense_m), (open_x, dense_x), (open_y, dense_y)):
        for t in range(EXT // 8):
            for b in range(LON // 128):
                piece = wide_m[t * 8 : (t + 1) * 8, b * 128 : (b + 1) * 128]
                for p in range(2):
                    dense[pl.ds(t * 64 + b * 2 + p, 8, stride=8), :] = piece

    for g, runs in enumerate(GROUPS):
        for b in range(LON // 128):
            lines = [
                jnp.broadcast_to(open_x[e : e + 1, b * 128 : (b + 1) * 128], (MAIN, 128)) for run in runs for e in run
            ]
            turned_open[g, b * 128 : (b + 1) * 128, :] = jnp.concatenate(lines, axis=0).T

    recv_rows = recv.reshape(PEERS * MINE, BLOCK)

    edge_rows = (0, 1, 2, 3, ROWS - 4, ROWS - 3, ROWS - 2, ROWS - 1)
    inner_rows = tuple(range(4, ROWS - 4))

    def place(z, rows, with_tail):
        ids = rowid[z]
        starts = [(z * GROUP + q) * MINE for q in range(GROUP)]
        main = jnp.concatenate([recv_rows[pl.ds(first, MAIN), :] for first in starts], axis=1)
        parts = [jnp.where(ids == 2 * r + half, main, bf16(0)) for r in rows for half in range(2)]
        if with_tail:
            rest = jnp.concatenate([recv_rows[pl.ds(first + MAIN, 2), :] for first in starts], axis=1)
            for p in range(2):
                line = jnp.broadcast_to(rest[p : p + 1], (ROWS, GROUP * BLOCK))
                parts += [jnp.where(ids == row_of + half, line, bf16(0)) for half in range(2)]
        left = jnp.concatenate(parts, axis=0)
        found = lax.dot_general(left, cols[z], (((1,), (1,)), ((), ())), preferred_element_type=f32)
        for i, r in enumerate(rows):
            for half in range(2):
                field[4 + r, :, half * HALF : (half + 1) * HALF] += found[(2 * i + half) * MAIN : (2 * i + half + 1) * MAIN]
        if with_tail:
            first = 2 * len(rows) * MAIN
            for half in range(2):
                for p in range(2):
                    start = first + (2 * p + half) * ROWS
                    tail[p * ROWS : (p + 1) * ROWS, half * HALF : (half + 1) * HALF] += found[start : start + ROWS]

    def arrive(z, count):
        block = recv.at[pl.ds(z * GROUP, count)]
        pltpu.make_async_copy(block, block, recv_sem.at[z]).wait()

    def place_both(k, carry):
        place(z_of(k), edge_rows, True)
        place(z_of(k), inner_rows, False)
        return carry

    def place_edges(k, carry):
        arrive(z_of(k), GROUP)
        place(z_of(k), edge_rows, True)
        return carry

    own.wait()
    arrive(mz, GROUP - 1)
    arrive(z_of(0), GROUP)
    lax.fori_loop(0, 2, place_both, 0)
    lax.fori_loop(2, NZ, place_edges, 0)

    forward = lax.rem(me, 2) == 0
    downstream = jnp.where(forward, upper, lower)
    upstream = jnp.where(forward, lower, upper)

    def pack(i, r):
        edge_out[i, :, :] = field[4 + r : 6 + r].reshape(2 * MAIN, LON).astype(bf16)
        pieces = [tail[p * ROWS + r : p * ROWS + r + 2, b * 128 : (b + 1) * 128] for b in range(LON // 128) for p in range(2)]
        tail_out[i, :, :] = jnp.concatenate(pieces, axis=0).astype(bf16)

    pack(0, ROWS - 2)
    pack(1, 0)

    def pack_first(r):
        pieces = [field[e, 0:1, b * 128 : (b + 1) * 128] for b in range(LON // 128) for e in (4 + r, 5 + r)]
        tail_out[3, :, :] = jnp.concatenate(pieces + [jnp.zeros((8, 128), f32)], axis=0).astype(bf16)

    @pl.when(forward)
    def _():
        pack(2, ROWS - 4)
        pack_first(2)

    @pl.when(jnp.logical_not(forward))
    def _():
        pack(2, 2)
        pack_first(ROWS - 4)

    edge_copies = []
    for i, other in enumerate((upper, lower, downstream, upstream)):
        for j, (src, dst) in enumerate(((edge_out, edge_in), (tail_out, tail_in))):
            if i == 3 and j == 0:
                continue
            copy = pltpu.make_async_remote_copy(
                src_ref=src.at[i],
                dst_ref=dst.at[i],
                send_sem=edge_send.at[i, j],
                recv_sem=edge_recv.at[i, j],
                device_id={"lat": other},
                device_id_type=MESH,
            )
            copy.start()
            edge_copies.append(copy)

    lax.fori_loop(2, NZ, lambda k, c: (place(z_of(k), inner_rows, False), c)[1], 0)

    for p in range(2):
        for b in range(LON // 128):
            for t in range(2):
                tail_d[pl.ds(32 + t * 64 + b * 2 + p, 8, stride=8), :] = tail[
                    p * ROWS + t * 8 : p * ROWS + t * 8 + 8, b * 128 : (b + 1) * 128
                ]

    def change_x(src, rows, g):
        blocks = []
        for b in range(LON // 128):
            blocks.append(jnp.concatenate([src[e, :, b * 128 : (b + 1) * 128] for e in rows], axis=0).T)
        now = jnp.concatenate(blocks, axis=0)

        def tiles(x):
            return x.reshape(LON // 8, 8, 128)

        ahead, far, here, there = turned_x
        side = jnp.where(ahead, tiles(pltpu.roll(now, 1, 0)), tiles(pltpu.roll(now, LON - 2, 0)))
        east = far * side + here * tiles(now) + there * tiles(pltpu.roll(now, LON - 1, 0))
        east = (east * tiles(turned_open[g])).reshape(LON, 128)
        change = east - pltpu.roll(east, 1, 0)
        back = [change[b * 128 : (b + 1) * 128].T for b in range(LON // 128)]
        return {e: jnp.concatenate([x[i * MAIN : (i + 1) * MAIN] for x in back], axis=1) for i, e in enumerate(rows)}

    def advance(src, runs, store):
        moved = change_x(src, [e for run in runs for e in run], GROUPS.index(runs))
        ahead, far, here, there = main_y

        def flux_y(e):
            side = jnp.where(ahead, src[e - 1], src[e + 2])
            return (far * side + here * src[e] + there * src[e + 1]) * open_y[e : e + 1, :]

        for run in runs:
            south = flux_y(run[0] - 1)
            for e in run:
                north = flux_y(e)
                store(e, (src[e] - moved[e] - (north - south)) * mask_x[e : e + 1, :])
                south = north

    def keep(e, new):
        mid[e] = new

    def finish(e, new):
        for h in range(MAIN // 8):
            for b in range(LON // 128):
                out_v[b, pl.ds(h * 8 * ROWS + e - 4, 8, stride=ROWS), :] = new[h * 8 : h * 8 + 8, b * 128 : (b + 1) * 128]

    lane3 = lax.broadcasted_iota(jnp.int32, (1, 8, 128), 2)

    def west_of(x):
        turned = pltpu.roll(x, 1, 2)
        return jnp.where(lane3 == 0, pltpu.roll(turned, 2, 1), turned)

    def east_of(x, n):
        turned = pltpu.roll(x, 128 - n, 2)
        return jnp.where(lane3 >= 128 - n, pltpu.roll(turned, 6, 1), turned)

    def rows3(ref, start, count):
        return ref[start * 8 : (start + count) * 8, :].reshape(count, 8, 128)

    def advance_tail(full, first):
        count = full.shape[0] - 4
        now = full[2 : count + 2]
        ahead, far, here, there = tail_x
        side = jnp.where(ahead, west_of(now), east_of(now, 2))
        east = (far * side + here * now + there * east_of(now, 1)) * rows3(dense_x, first + 2, count)
        ahead, far, here, there = tail_y
        side = jnp.where(ahead, full[0 : count + 1], full[3 : count + 4])
        north = (far * side + here * full[1 : count + 2] + there * full[2 : count + 3]) * rows3(
            dense_y, first + 1, count + 1
        )
        return (now - (east - west_of(east)) - (north[1:] - north[:-1])) * rows3(dense_m, first + 2, count)

    for runs in FIRST_INNER:
        advance(field, runs, keep)
    for runs in SECOND_INNER:
        advance(mid, runs, finish)
    tail_half = advance_tail(rows3(tail_d, 4, ROWS), 4)
    tail_mid[48:144, :] = tail_half.reshape(96, 128)
    tail_done[32:96, :] = advance_tail(tail_half, 6).reshape(64, 128)

    for copy in edge_copies:
        copy.wait()
    def unpack(i, e, there):
        field[e : e + 2] = (edge_in[i].astype(f32) * there).reshape(2, MAIN, LON)
        ghost = tail_in[i].astype(f32) * there
        for k in range(8):
            tail_d[pl.ds(e * 8 + k, 2, stride=8), :] = ghost[2 * k : 2 * k + 2]

    unpack(0, 2, has_lower)
    unpack(1, EXT - 4, has_upper)

    def unpack_first(e, there):
        ghost = tail_in[3].astype(f32) * there
        for b in range(LON // 128):
            for i in range(2):
                field[e + i, 0:1, b * 128 : (b + 1) * 128] = ghost[2 * b + i : 2 * b + i + 1]

    @pl.when(forward)
    def _():
        unpack(2, 0, has_lower)
        unpack_first(EXT - 2, has_upper)

    @pl.when(jnp.logical_not(forward))
    def _():
        unpack(2, EXT - 2, has_upper)
        unpack_first(0, has_lower)

    for runs in FIRST_OUTER:
        advance(field, runs, keep)
    for runs in SECOND_OUTER:
        advance(mid, runs, finish)
    low = jnp.concatenate([advance_tail(rows3(tail_d, 0, 8), 0), rows3(tail_mid, 6, 4)], axis=0)
    tail_done[0:32, :] = advance_tail(low, 2).reshape(32, 128)
    high = jnp.concatenate([rows3(tail_mid, 14, 4), advance_tail(rows3(tail_d, 16, 8), 16)], axis=0)
    tail_done[96:128, :] = advance_tail(high, 14).reshape(32, 128)

    for b in range(LON // 128):
        out[: MAIN * ROWS, b * 128 : (b + 1) * 128] = out_v[b]
        for p in range(2):
            out[(MAIN + p) * ROWS : (MAIN + p + 1) * ROWS, b * 128 : (b + 1) * 128] = tail_done[
                pl.ds(b * 2 + p, ROWS, stride=8), :
            ]
    sent = send.at[pl.ds(0, PEERS - 1)]
    pltpu.make_async_copy(sent, sent, send_sem).wait()


def body(spectrum, sea_cells, sea_count, refraction, wind_speed, growth, damping, courant):
    vmem, smem, dma = pltpu.VMEM, pltpu.SMEM, pltpu.SemaphoreType.DMA
    table = jnp.asarray(direction_table())
    block = (PEERS, MINE // 2, 2, BLOCK)
    scratch = [
        vmem((NCOMP, BLOCK), bf16),
        vmem((1, SLOTS), jnp.int32),
        vmem((1, BLOCK), f32),
        vmem((1, BLOCK), f32),
        vmem((NCOMP,), f32),
        vmem((NCOMP,), f32),
        smem((32,), f32),
        vmem((2, 32, 128), f32),
        vmem((NCOMP, BLOCK), f32),
        vmem((NCOMP, BLOCK), f32),
        vmem((NCOMP, BLOCK), f32),
        vmem(block, bf16),
        vmem(block, bf16),
        vmem((NZ, HALF, GROUP * BLOCK), bf16),
        vmem((NZ, ROWS, GROUP * BLOCK), jnp.int16),
        vmem((ROWS, LON), bf16),
        vmem((2, ROWS, LON), bf16),
        vmem((EXT, LON), f32),
        vmem((EXT, LON), f32),
        vmem((EXT, LON), f32),
        vmem((len(GROUPS), LON, 128), f32),
        vmem((EXT * 8, 128), f32),
        vmem((EXT * 8, 128), f32),
        vmem((EXT * 8, 128), f32),
        vmem((EXT, MAIN, LON), f32),
        vmem((EXT, MAIN, LON), f32),
        vmem((2 * ROWS, LON), f32),
        vmem((EXT * 8, 128), f32),
        vmem((EXT * 8, 128), f32),
        vmem((ROWS * 8, 128), f32),
        vmem((3, 2 * MAIN, LON), bf16),
        vmem((3, 2 * MAIN, LON), bf16),
        vmem((4, 16, 128), bf16),
        vmem((4, 16, 128), bf16),
        vmem((LON // 128, MAIN * ROWS, 128), f32),
        dma((8,)),
        dma,
        dma((NZ,)),
        dma,
        dma((2,)),
        dma((2,)),
        dma((4, 2)),
        dma((4, 2)),
    ]
    inputs = (spectrum, sea_cells, sea_count, refraction, wind_speed, growth, damping, courant, table)
    out = pl.pallas_call(
        kernel,
        out_shape=jax.ShapeDtypeStruct((MINE * ROWS, LON), f32),
        in_specs=[pl.BlockSpec(memory_space=pltpu.SMEM if x is sea_count else pltpu.HBM) for x in inputs],
        out_specs=pl.BlockSpec(memory_space=pltpu.VMEM),
        scratch_shapes=scratch,
        compiler_params=pltpu.CompilerParams(collective_id=0, has_side_effects=True, vmem_limit_bytes=40 << 20),
        name="wave_step",
    )(*[x if x is sea_count else pltpu.with_memory_space_constraint(x, pltpu.HBM) for x in inputs])
    return out.reshape(MINE, ROWS, LON)


def solution(mesh):
    return jax.shard_map(
        body,
        mesh=mesh,
        in_specs=(
            P(None, ("lat", "comp")),
            P("lat", None),
            P("lat"),
            P("lat", None),
            P("lat", None),
            P(),
            P(),
            P(),
        ),
        out_specs=P("comp", "lat", None),
        check_vma=False,
    )
```

```python
import math

import jax
import jax.numpy as jnp
import numpy as np
from jax import lax
from jax.experimental import pallas as pl
from jax.experimental.pallas import tpu as pltpu
from jax.sharding import PartitionSpec as P

MESH = pl.DeviceIdType.MESH
NDIR = 36
NCOMP = 1152
ROWS = 16
LON = 512
HALF = LON // 2
BATCH = 2
TILES = 8
SLOTS = 8192
PEERS = 64
NX, NZ, NCORE = 4, 8, 2
GROUP = NX * NCORE
BLOCK = 128
MINE = NCOMP // PEERS
MAIN = 16
EXT = ROWS + 8
CHUNK = 4 * NDIR

f32 = jnp.float32
bf16 = jnp.bfloat16


FIRST_INNER = ((range(6, 14),), (range(10, 18),))
FIRST_OUTER = ((range(2, 6), range(18, 22)),)
SECOND_INNER = ((range(8, 16),),)
SECOND_OUTER = ((range(4, 8), range(16, 20)),)
GROUPS = FIRST_INNER + FIRST_OUTER + SECOND_INNER + SECOND_OUTER


def direction_table():
    angles = np.arange(NDIR, dtype=np.float32) * np.float32(2.0 * math.pi / NDIR)
    pick = list(range(MAIN)) + [MAIN, MAIN + 1] * 4
    table = np.zeros((2, 2, 32, 128), np.float32)
    for half in range(2):
        rows = angles[half * MINE + np.array(pick)]
        across = np.tile(angles[half * MINE : half * MINE + MAIN], 128 // MAIN)
        for i, wave in enumerate((np.cos, np.sin)):
            table[half, i, :24] = wave(rows)[:, None]
            table[half, i, 24:] = wave(across)[None, :]
    return table


def face_weights(speed):
    size = jnp.abs(speed)
    third = (1.0 - speed * speed) / 6.0
    near = (0.5 + 0.5 * size + 2.0 * third) * speed
    far = (0.5 - 0.5 * size - third) * speed
    ahead = speed >= 0.0
    return ahead, -third * speed, jnp.where(ahead, near, far), jnp.where(ahead, far, near)


def kernel(
    spec_hbm, cells_hbm, count_s, refr_hbm, wind_hbm, growth_hbm, damp_hbm, cour_hbm, table_hbm, out,
    spec_v, cells_v, refr_v, wind_v, growth_v, damp_v, cour_s, table_v,
    growth_b, damp_b, bent, send, recv, cols, rowid, mask_bf, mask_in,
    mask_x, open_x, open_y, turned_open, dense_m, dense_x, dense_y,
    field, mid, tail, tail_d, tail_mid, tail_done, edge_out, edge_in, tail_out, tail_in, out_v,
    in_sem, send_sem, recv_sem, own_sem, mask_send, mask_recv, edge_send, edge_recv,
):
    me = lax.axis_index("comp")
    lat = lax.axis_index("lat")
    mx, mz, mc = lax.div(me, NZ * NCORE), lax.div(lax.rem(me, NZ * NCORE), NCORE), lax.rem(me, NCORE)
    mq = mx * NCORE + mc
    upper, lower = lax.rem(lat + 1, TILES), lax.rem(lat + TILES - 1, TILES)

    barrier = pltpu.get_barrier_semaphore()

    def for_peers(act):
        def group(z, carry):
            q = mq
            for j in range(GROUP):
                other = lax.div(q, NCORE) * (NZ * NCORE) + lax.rem(q, NCORE) + z * NCORE
                if j == 0:
                    pl.when(z != mz)(lambda other=other: act(other))
                else:
                    act(other)
                q = jnp.where(q == GROUP - 1, 0, q + 1)
            return carry

        lax.fori_loop(0, NZ, group, 0)

    def greet(other):
        pl.semaphore_signal(barrier, inc=1, device_id={"comp": other}, device_id_type=MESH)

    for_peers(greet)
    for other in (upper, lower):
        pl.semaphore_signal(barrier, inc=1, device_id={"lat": other}, device_id_type=MESH)

    my_slots = pl.ds(pl.multiple_of(me * BLOCK, BLOCK), BLOCK)
    loads = [
        (spec_hbm, spec_v),
        (cells_hbm, cells_v),
        (refr_hbm.at[:, my_slots], refr_v),
        (wind_hbm.at[:, my_slots], wind_v),
        (growth_hbm, growth_v),
        (damp_hbm, damp_v),
        (cour_hbm, cour_s),
        (table_hbm.at[lax.rem(me, 2)], table_v),
    ]
    copies = [pltpu.make_async_copy(src, dst, in_sem.at[i]) for i, (src, dst) in enumerate(loads)]
    for copy in copies:
        copy.start()
    for copy in copies:
        copy.wait()

    for j in range(NCOMP // 128):
        part = pl.ds(j * 128, 128)
        growth_b[part, :] = jnp.broadcast_to(growth_v[part].reshape(1, 128), (128, 128)).T
        damp_b[part, :] = jnp.broadcast_to(damp_v[part].reshape(1, 128), (128, 128)).T

    bend = refr_v[...]
    bend_up = jnp.broadcast_to(jnp.maximum(bend, 0.0), (CHUNK, BLOCK))
    bend_down = jnp.broadcast_to(jnp.maximum(-bend, 0.0), (CHUNK, BLOCK))
    dir_of = lax.rem(lax.broadcasted_iota(jnp.int32, (CHUNK, BLOCK), 0), NDIR)

    def refract(g, total):
        part = pl.ds(pl.multiple_of(g * CHUNK, CHUNK), CHUNK)
        energy = spec_v[part, :].astype(f32)
        before = jnp.where(dir_of == 0, pltpu.roll(energy, CHUNK - NDIR + 1, 0), pltpu.roll(energy, 1, 0))
        after = jnp.where(dir_of == NDIR - 1, pltpu.roll(energy, NDIR - 1, 0), pltpu.roll(energy, CHUNK - 1, 0))
        moved = energy + bend_up * (before - energy) + bend_down * (after - energy)
        bent[part, :] = moved
        return total + jnp.sum(moved.reshape(CHUNK // 8, 8, BLOCK), axis=0)

    total = lax.fori_loop(0, NCOMP // CHUNK, refract, jnp.zeros((8, BLOCK), f32))
    mean = jnp.sum(total, axis=0, keepdims=True) / NCOMP
    loss = jnp.broadcast_to(mean / (mean + 1.0), (CHUNK, BLOCK))
    wind = jnp.broadcast_to(wind_v[...], (CHUNK, BLOCK))
    send_rows = send.reshape(NCOMP, BLOCK)

    def source(g, carry):
        part = pl.ds(pl.multiple_of(g * CHUNK, CHUNK), CHUNK)
        rate = growth_b[part, :] * wind - damp_b[part, :] * loss
        send_rows[part, :] = (bent[part, :] * jnp.exp(rate)).astype(bf16)
        return carry

    lax.fori_loop(0, NCOMP // CHUNK, source, 0)

    pl.semaphore_wait(barrier, PEERS - 1 + 2)

    def give(other):
        pltpu.make_async_remote_copy(
            src_ref=send.at[other],
            dst_ref=recv.at[mz * GROUP + mq],
            send_sem=send_sem,
            recv_sem=recv_sem.at[mz],
            device_id={"comp": other},
            device_id_type=MESH,
        ).start()

    for_peers(give)
    own = pltpu.make_async_copy(send.at[me], recv.at[mz * GROUP + mq], own_sem)
    own.start()

    live_count = count_s[0]
    lane = lax.broadcasted_iota(jnp.int32, (1, BLOCK), 1)
    col_of = lax.broadcasted_iota(jnp.int16, (HALF, BLOCK), 0)
    row_of = 2 * lax.broadcasted_iota(jnp.int16, (ROWS, GROUP * BLOCK), 0)

    def factors(z, total):
        for q in range(GROUP):
            first = ((q // NCORE) * (NZ * NCORE) + z * NCORE + q % NCORE) * BLOCK
            cell = cells_v[:, pl.ds(pl.multiple_of(first, BLOCK), BLOCK)]
            col = jnp.broadcast_to(lax.bitwise_and(cell, HALF - 1), (HALF, BLOCK)).astype(jnp.int16)
            cols[z, :, q * BLOCK : (q + 1) * BLOCK] = jnp.where(col_of == col, bf16(1), bf16(0))
            row = jnp.where(lane + first < live_count, lax.shift_right_logical(cell, 8), 2 * ROWS)
            rowid[z, :, q * BLOCK : (q + 1) * BLOCK] = jnp.broadcast_to(row, (ROWS, BLOCK)).astype(jnp.int16)
        ids = rowid[z]
        hot = jnp.concatenate([jnp.where(ids == row_of + half, bf16(1), bf16(0)) for half in range(2)], axis=0)
        return total + lax.dot_general(hot, cols[z], (((1,), (1,)), ((), ())), preferred_element_type=f32)

    mask = lax.fori_loop(0, NZ, factors, jnp.zeros((2 * ROWS, HALF), f32))
    mask = jnp.concatenate([mask[:ROWS], mask[ROWS:]], axis=1)
    mask_bf[...] = mask.astype(bf16)
    mask_copies = []
    for i, other in enumerate((upper, lower)):
        copy = pltpu.make_async_remote_copy(
            src_ref=mask_bf,
            dst_ref=mask_in.at[i],
            send_sem=mask_send.at[i],
            recv_sem=mask_recv.at[i],
            device_id={"lat": other},
            device_id_type=MESH,
        )
        copy.start()
        mask_copies.append(copy)

    field[...] = jnp.zeros_like(field)
    tail[...] = jnp.zeros_like(tail)
    tail_d[...] = jnp.zeros_like(tail_d)
    speed = cour_s[me // 2]
    wx = face_weights(speed * table_v[0])
    wy = face_weights(speed * table_v[1])

    def wide(x, first, count):
        return jnp.concatenate([x[first : first + count]] * (LON // 128), axis=1)

    main_y = [wide(w, 0, MAIN) for w in wy]
    turned_x = [w[24:][None] for w in wx]
    tail_x, tail_y = [[x[MAIN:24][None] for x in w] for w in (wx, wy)]

    for copy in mask_copies:
        copy.wait()
    has_lower = jnp.where(lat > 0, 1.0, 0.0)
    has_upper = jnp.where(lat < TILES - 1, 1.0, 0.0)
    below = mask_in[0].astype(f32)[ROWS - 4 :] * has_lower
    above = mask_in[1].astype(f32)[:4] * has_upper
    full = jnp.concatenate([below, mask, above], axis=0)
    mask_x[...] = full
    open_x[...] = full * pltpu.roll(full, LON - 1, 1)
    open_y[...] = full * pltpu.roll(full, EXT - 1, 0)
    for wide_m, dense in ((mask_x, dense_m), (open_x, dense_x), (open_y, dense_y)):
        for t in range(EXT // 8):
            for b in range(LON // 128):
                piece = wide_m[t * 8 : (t + 1) * 8, b * 128 : (b + 1) * 128]
                for p in range(2):
                    dense[pl.ds(t * 64 + b * 2 + p, 8, stride=8), :] = piece

    for g, runs in enumerate(GROUPS):
        for b in range(LON // 128):
            lines = [
                jnp.broadcast_to(open_x[e : e + 1, b * 128 : (b + 1) * 128], (MAIN, 128)) for run in runs for e in run
            ]
            turned_open[g, b * 128 : (b + 1) * 128, :] = jnp.concatenate(lines, axis=0).T

    recv_rows = recv.reshape(PEERS * MINE, BLOCK)

    edge_rows = (0, 1, 2, 3, ROWS - 4, ROWS - 3, ROWS - 2, ROWS - 1)
    inner_rows = tuple(range(4, ROWS - 4))

    def left_factor(z, rows, with_tail):
        ids = rowid[z]
        starts = [(z * GROUP + q) * MINE for q in range(GROUP)]
        main = jnp.concatenate([recv_rows[pl.ds(first, MAIN), :] for first in starts], axis=1)
        parts = [jnp.where(ids == 2 * r + half, main, bf16(0)) for r in rows for half in range(2)]
        if with_tail:
            rest = jnp.concatenate([recv_rows[pl.ds(first + MAIN, 2), :] for first in starts], axis=1)
            for p in range(2):
                line = jnp.broadcast_to(rest[p : p + 1], (ROWS, GROUP * BLOCK))
                parts += [jnp.where(ids == row_of + half, line, bf16(0)) for half in range(2)]
        return jnp.concatenate(parts, axis=0)

    def place(zs, rows, with_tail):
        left = jnp.concatenate([left_factor(z, rows, with_tail) for z in zs], axis=1)
        right = jnp.concatenate([cols[z] for z in zs], axis=1)
        found = lax.dot_general(left, right, (((1,), (1,)), ((), ())), preferred_element_type=f32)
        for i, r in enumerate(rows):
            for half in range(2):
                field[4 + r, :, half * HALF : (half + 1) * HALF] += found[(2 * i + half) * MAIN : (2 * i + half + 1) * MAIN]
        if with_tail:
            first = 2 * len(rows) * MAIN
            for half in range(2):
                for p in range(2):
                    start = first + (2 * p + half) * ROWS
                    tail[p * ROWS : (p + 1) * ROWS, half * HALF : (half + 1) * HALF] += found[start : start + ROWS]

    def arrive(z, count):
        block = recv.at[pl.ds(z * GROUP, count)]
        pltpu.make_async_copy(block, block, recv_sem.at[z]).wait()

    def z_of(k):
        steps = lax.div(k + 1, 2)
        return lax.rem(mz + jnp.where(lax.rem(k, 2) == 1, steps, NZ - steps), NZ)

    def place_edges(i, carry):
        zs = [z_of(i * BATCH + k) for k in range(BATCH)]

        @pl.when(i > 0)
        def _():
            arrive(zs[0], GROUP)

        for z in zs[1:]:
            arrive(z, GROUP)
        place(zs, edge_rows, True)
        return carry

    def place_inner(i, carry):
        place([i * BATCH + k for k in range(BATCH)], inner_rows, False)
        return carry

    own.wait()
    arrive(mz, GROUP - 1)
    lax.fori_loop(0, NZ // BATCH, place_edges, 0)

    forward = lax.rem(me, 2) == 0
    downstream = jnp.where(forward, upper, lower)
    upstream = jnp.where(forward, lower, upper)

    def pack(i, r):
        edge_out[i, :, :] = field[4 + r : 6 + r].reshape(2 * MAIN, LON).astype(bf16)
        pieces = [tail[p * ROWS + r : p * ROWS + r + 2, b * 128 : (b + 1) * 128] for b in range(LON // 128) for p in range(2)]
        tail_out[i, :, :] = jnp.concatenate(pieces, axis=0).astype(bf16)

    pack(0, ROWS - 2)
    pack(1, 0)

    def pack_first(r):
        pieces = [field[e, 0:1, b * 128 : (b + 1) * 128] for b in range(LON // 128) for e in (4 + r, 5 + r)]
        tail_out[3, :, :] = jnp.concatenate(pieces + [jnp.zeros((8, 128), f32)], axis=0).astype(bf16)

    @pl.when(forward)
    def _():
        pack(2, ROWS - 4)
        pack_first(2)

    @pl.when(jnp.logical_not(forward))
    def _():
        pack(2, 2)
        pack_first(ROWS - 4)

    edge_copies = []
    for i, other in enumerate((upper, lower, downstream, upstream)):
        for j, (src, dst) in enumerate(((edge_out, edge_in), (tail_out, tail_in))):
            if i == 3 and j == 0:
                continue
            copy = pltpu.make_async_remote_copy(
                src_ref=src.at[i],
                dst_ref=dst.at[i],
                send_sem=edge_send.at[i, j],
                recv_sem=edge_recv.at[i, j],
                device_id={"lat": other},
                device_id_type=MESH,
            )
            copy.start()
            edge_copies.append(copy)

    lax.fori_loop(0, NZ // BATCH, place_inner, 0)

    for p in range(2):
        for b in range(LON // 128):
            for t in range(2):
                tail_d[pl.ds(32 + t * 64 + b * 2 + p, 8, stride=8), :] = tail[
                    p * ROWS + t * 8 : p * ROWS + t * 8 + 8, b * 128 : (b + 1) * 128
                ]

    def change_x(src, rows, g):
        blocks = []
        for b in range(LON // 128):
            blocks.append(jnp.concatenate([src[e, :, b * 128 : (b + 1) * 128] for e in rows], axis=0).T)
        now = jnp.concatenate(blocks, axis=0)

        def tiles(x):
            return x.reshape(LON // 8, 8, 128)

        ahead, far, here, there = turned_x
        side = jnp.where(ahead, tiles(pltpu.roll(now, 1, 0)), tiles(pltpu.roll(now, LON - 2, 0)))
        east = far * side + here * tiles(now) + there * tiles(pltpu.roll(now, LON - 1, 0))
        east = (east * tiles(turned_open[g])).reshape(LON, 128)
        change = east - pltpu.roll(east, 1, 0)
        back = [change[b * 128 : (b + 1) * 128].T for b in range(LON // 128)]
        return {e: jnp.concatenate([x[i * MAIN : (i + 1) * MAIN] for x in back], axis=1) for i, e in enumerate(rows)}

    def advance(src, runs, store):
        moved = change_x(src, [e for run in runs for e in run], GROUPS.index(runs))
        ahead, far, here, there = main_y

        def flux_y(e):
            side = jnp.where(ahead, src[e - 1], src[e + 2])
            return (far * side + here * src[e] + there * src[e + 1]) * open_y[e : e + 1, :]

        for run in runs:
            south = flux_y(run[0] - 1)
            for e in run:
                north = flux_y(e)
                store(e, (src[e] - moved[e] - (north - south)) * mask_x[e : e + 1, :])
                south = north

    def keep(e, new):
        mid[e] = new

    def finish(e, new):
        for h in range(MAIN // 8):
            for b in range(LON // 128):
                out_v[b, pl.ds(h * 8 * ROWS + e - 4, 8, stride=ROWS), :] = new[h * 8 : h * 8 + 8, b * 128 : (b + 1) * 128]

    lane3 = lax.broadcasted_iota(jnp.int32, (1, 8, 128), 2)

    def west_of(x):
        turned = pltpu.roll(x, 1, 2)
        return jnp.where(lane3 == 0, pltpu.roll(turned, 2, 1), turned)

    def east_of(x, n):
        turned = pltpu.roll(x, 128 - n, 2)
        return jnp.where(lane3 >= 128 - n, pltpu.roll(turned, 6, 1), turned)

    def rows3(ref, start, count):
        return ref[start * 8 : (start + count) * 8, :].reshape(count, 8, 128)

    def advance_tail(full, first):
        count = full.shape[0] - 4
        now = full[2 : count + 2]
        ahead, far, here, there = tail_x
        side = jnp.where(ahead, west_of(now), east_of(now, 2))
        east = (far * side + here * now + there * east_of(now, 1)) * rows3(dense_x, first + 2, count)
        ahead, far, here, there = tail_y
        side = jnp.where(ahead, full[0 : count + 1], full[3 : count + 4])
        north = (far * side + here * full[1 : count + 2] + there * full[2 : count + 3]) * rows3(
            dense_y, first + 1, count + 1
        )
        return (now - (east - west_of(east)) - (north[1:] - north[:-1])) * rows3(dense_m, first + 2, count)

    for runs in FIRST_INNER:
        advance(field, runs, keep)
    for runs in SECOND_INNER:
        advance(mid, runs, finish)
    tail_half = advance_tail(rows3(tail_d, 4, ROWS), 4)
    tail_mid[48:144, :] = tail_half.reshape(96, 128)
    tail_done[32:96, :] = advance_tail(tail_half, 6).reshape(64, 128)

    for copy in edge_copies:
        copy.wait()
    def unpack(i, e, there):
        field[e : e + 2] = (edge_in[i].astype(f32) * there).reshape(2, MAIN, LON)
        ghost = tail_in[i].astype(f32) * there
        for k in range(8):
            tail_d[pl.ds(e * 8 + k, 2, stride=8), :] = ghost[2 * k : 2 * k + 2]

    unpack(0, 2, has_lower)
    unpack(1, EXT - 4, has_upper)

    def unpack_first(e, there):
        ghost = tail_in[3].astype(f32) * there
        for b in range(LON // 128):
            for i in range(2):
                field[e + i, 0:1, b * 128 : (b + 1) * 128] = ghost[2 * b + i : 2 * b + i + 1]

    @pl.when(forward)
    def _():
        unpack(2, 0, has_lower)
        unpack_first(EXT - 2, has_upper)

    @pl.when(jnp.logical_not(forward))
    def _():
        unpack(2, EXT - 2, has_upper)
        unpack_first(0, has_lower)

    for runs in FIRST_OUTER:
        advance(field, runs, keep)
    for runs in SECOND_OUTER:
        advance(mid, runs, finish)
    low = jnp.concatenate([advance_tail(rows3(tail_d, 0, 8), 0), rows3(tail_mid, 6, 4)], axis=0)
    tail_done[0:32, :] = advance_tail(low, 2).reshape(32, 128)
    high = jnp.concatenate([rows3(tail_mid, 14, 4), advance_tail(rows3(tail_d, 16, 8), 16)], axis=0)
    tail_done[96:128, :] = advance_tail(high, 14).reshape(32, 128)

    for b in range(LON // 128):
        out[: MAIN * ROWS, b * 128 : (b + 1) * 128] = out_v[b]
        for p in range(2):
            out[(MAIN + p) * ROWS : (MAIN + p + 1) * ROWS, b * 128 : (b + 1) * 128] = tail_done[
                pl.ds(b * 2 + p, ROWS, stride=8), :
            ]
    sent = send.at[pl.ds(0, PEERS - 1)]
    pltpu.make_async_copy(sent, sent, send_sem).wait()


def body(spectrum, sea_cells, sea_count, refraction, wind_speed, growth, damping, courant):
    vmem, smem, dma = pltpu.VMEM, pltpu.SMEM, pltpu.SemaphoreType.DMA
    table = jnp.asarray(direction_table())
    block = (PEERS, MINE // 2, 2, BLOCK)
    scratch = [
        vmem((NCOMP, BLOCK), bf16),
        vmem((1, SLOTS), jnp.int32),
        vmem((1, BLOCK), f32),
        vmem((1, BLOCK), f32),
        vmem((NCOMP,), f32),
        vmem((NCOMP,), f32),
        smem((32,), f32),
        vmem((2, 32, 128), f32),
        vmem((NCOMP, BLOCK), f32),
        vmem((NCOMP, BLOCK), f32),
        vmem((NCOMP, BLOCK), f32),
        vmem(block, bf16),
        vmem(block, bf16),
        vmem((NZ, HALF, GROUP * BLOCK), bf16),
        vmem((NZ, ROWS, GROUP * BLOCK), jnp.int16),
        vmem((ROWS, LON), bf16),
        vmem((2, ROWS, LON), bf16),
        vmem((EXT, LON), f32),
        vmem((EXT, LON), f32),
        vmem((EXT, LON), f32),
        vmem((len(GROUPS), LON, 128), f32),
        vmem((EXT * 8, 128), f32),
        vmem((EXT * 8, 128), f32),
        vmem((EXT * 8, 128), f32),
        vmem((EXT, MAIN, LON), f32),
        vmem((EXT, MAIN, LON), f32),
        vmem((2 * ROWS, LON), f32),
        vmem((EXT * 8, 128), f32),
        vmem((EXT * 8, 128), f32),
        vmem((ROWS * 8, 128), f32),
        vmem((3, 2 * MAIN, LON), bf16),
        vmem((3, 2 * MAIN, LON), bf16),
        vmem((4, 16, 128), bf16),
        vmem((4, 16, 128), bf16),
        vmem((LON // 128, MAIN * ROWS, 128), f32),
        dma((8,)),
        dma,
        dma((NZ,)),
        dma,
        dma((2,)),
        dma((2,)),
        dma((4, 2)),
        dma((4, 2)),
    ]
    inputs = (spectrum, sea_cells, sea_count, refraction, wind_speed, growth, damping, courant, table)
    out = pl.pallas_call(
        kernel,
        out_shape=jax.ShapeDtypeStruct((MINE * ROWS, LON), f32),
        in_specs=[pl.BlockSpec(memory_space=pltpu.SMEM if x is sea_count else pltpu.HBM) for x in inputs],
        out_specs=pl.BlockSpec(memory_space=pltpu.VMEM),
        scratch_shapes=scratch,
        compiler_params=pltpu.CompilerParams(collective_id=0, has_side_effects=True, vmem_limit_bytes=40 << 20),
        name="wave_step",
    )(*[x if x is sea_count else pltpu.with_memory_space_constraint(x, pltpu.HBM) for x in inputs])
    return out.reshape(MINE, ROWS, LON)


def solution(mesh):
    return jax.shard_map(
        body,
        mesh=mesh,
        in_specs=(
            P(None, ("lat", "comp")),
            P("lat", None),
            P("lat"),
            P("lat", None),
            P("lat", None),
            P(),
            P(),
            P(),
        ),
        out_specs=P("comp", "lat", None),
        check_vma=False,
    )
```

```python
import math

import jax
import jax.numpy as jnp
import numpy as np
from jax import lax
from jax.experimental import pallas as pl
from jax.experimental.pallas import tpu as pltpu
from jax.sharding import PartitionSpec as P

MESH = pl.DeviceIdType.MESH
NDIR = 36
NCOMP = 1152
ROWS = 16
LON = 512
HALF = LON // 2
BATCH = 2
TILES = 8
SLOTS = 8192
PEERS = 64
NX, NZ, NCORE = 4, 8, 2
GROUP = NX * NCORE
BLOCK = 128
MINE = NCOMP // PEERS
MAIN = 16
EXT = ROWS + 8
CHUNK = 4 * NDIR

f32 = jnp.float32
bf16 = jnp.bfloat16


FIRST_INNER = ((range(6, 14),), (range(10, 18),))
FIRST_OUTER = ((range(2, 6), range(18, 22)),)
SECOND_INNER = ((range(8, 16),),)
SECOND_OUTER = ((range(4, 8), range(16, 20)),)
GROUPS = FIRST_INNER + FIRST_OUTER + SECOND_INNER + SECOND_OUTER


def direction_table():
    angles = np.arange(NDIR, dtype=np.float32) * np.float32(2.0 * math.pi / NDIR)
    pick = list(range(MAIN)) + [MAIN, MAIN + 1] * 4
    table = np.zeros((2, 2, 32, 128), np.float32)
    for half in range(2):
        rows = angles[half * MINE + np.array(pick)]
        across = np.tile(angles[half * MINE : half * MINE + MAIN], 128 // MAIN)
        for i, wave in enumerate((np.cos, np.sin)):
            table[half, i, :24] = wave(rows)[:, None]
            table[half, i, 24:] = wave(across)[None, :]
    return table


def face_weights(speed):
    size = jnp.abs(speed)
    third = (1.0 - speed * speed) / 6.0
    near = (0.5 + 0.5 * size + 2.0 * third) * speed
    far = (0.5 - 0.5 * size - third) * speed
    ahead = speed >= 0.0
    return ahead, -third * speed, jnp.where(ahead, near, far), jnp.where(ahead, far, near)


def kernel(
    spec_hbm, cells_hbm, count_hbm, refr_hbm, wind_hbm, growth_hbm, damp_hbm, cour_hbm, table_hbm, out,
    spec_v, cells_v, count_v, refr_v, wind_v, growth_v, damp_v, cour_s, table_v,
    growth_b, damp_b, bent, send, recv, cols, rowid, mask_bf, mask_in,
    mask_x, open_x, open_y, turned_open, dense_m, dense_x, dense_y,
    field, mid, tail, tail_d, tail_mid, tail_done, edge_out, edge_in, tail_out, tail_in, out_v,
    in_sem, send_sem, recv_sem, own_sem, mask_send, mask_recv, edge_send, edge_recv,
):
    me = lax.axis_index("comp")
    lat = lax.axis_index("lat")
    mx, mz, mc = lax.div(me, NZ * NCORE), lax.div(lax.rem(me, NZ * NCORE), NCORE), lax.rem(me, NCORE)
    mq = mx * NCORE + mc
    upper, lower = lax.rem(lat + 1, TILES), lax.rem(lat + TILES - 1, TILES)

    barrier = pltpu.get_barrier_semaphore()

    def for_peers(act):
        def group(z, carry):
            q = mq
            for j in range(GROUP):
                other = lax.div(q, NCORE) * (NZ * NCORE) + lax.rem(q, NCORE) + z * NCORE
                if j == 0:
                    pl.when(z != mz)(lambda other=other: act(other))
                else:
                    act(other)
                q = jnp.where(q == GROUP - 1, 0, q + 1)
            return carry

        lax.fori_loop(0, NZ, group, 0)

    def greet(other):
        pl.semaphore_signal(barrier, inc=1, device_id={"comp": other}, device_id_type=MESH)

    for_peers(greet)
    for other in (upper, lower):
        pl.semaphore_signal(barrier, inc=1, device_id={"lat": other}, device_id_type=MESH)

    my_slots = pl.ds(pl.multiple_of(me * BLOCK, BLOCK), BLOCK)
    loads = [
        (spec_hbm, spec_v),
        (cells_hbm, cells_v),
        (count_hbm, count_v),
        (refr_hbm.at[:, my_slots], refr_v),
        (wind_hbm.at[:, my_slots], wind_v),
        (growth_hbm, growth_v),
        (damp_hbm, damp_v),
        (cour_hbm, cour_s),
        (table_hbm.at[lax.rem(me, 2)], table_v),
    ]
    copies = [pltpu.make_async_copy(src, dst, in_sem.at[i]) for i, (src, dst) in enumerate(loads)]
    for copy in copies:
        copy.start()
    for copy in copies:
        copy.wait()

    for j in range(NCOMP // 128):
        part = pl.ds(j * 128, 128)
        growth_b[part, :] = jnp.broadcast_to(growth_v[part].reshape(1, 128), (128, 128)).T
        damp_b[part, :] = jnp.broadcast_to(damp_v[part].reshape(1, 128), (128, 128)).T

    bend = refr_v[...]
    bend_up = jnp.broadcast_to(jnp.maximum(bend, 0.0), (CHUNK, BLOCK))
    bend_down = jnp.broadcast_to(jnp.maximum(-bend, 0.0), (CHUNK, BLOCK))
    dir_of = lax.rem(lax.broadcasted_iota(jnp.int32, (CHUNK, BLOCK), 0), NDIR)

    def refract(g, total):
        part = pl.ds(pl.multiple_of(g * CHUNK, CHUNK), CHUNK)
        energy = spec_v[part, :].astype(f32)
        before = jnp.where(dir_of == 0, pltpu.roll(energy, CHUNK - NDIR + 1, 0), pltpu.roll(energy, 1, 0))
        after = jnp.where(dir_of == NDIR - 1, pltpu.roll(energy, NDIR - 1, 0), pltpu.roll(energy, CHUNK - 1, 0))
        moved = energy + bend_up * (before - energy) + bend_down * (after - energy)
        bent[part, :] = moved
        return total + jnp.sum(moved.reshape(CHUNK // 8, 8, BLOCK), axis=0)

    total = lax.fori_loop(0, NCOMP // CHUNK, refract, jnp.zeros((8, BLOCK), f32))
    mean = jnp.sum(total, axis=0, keepdims=True) / NCOMP
    loss = jnp.broadcast_to(mean / (mean + 1.0), (CHUNK, BLOCK))
    wind = jnp.broadcast_to(wind_v[...], (CHUNK, BLOCK))
    send_rows = send.reshape(NCOMP, BLOCK)

    def source(g, carry):
        part = pl.ds(pl.multiple_of(g * CHUNK, CHUNK), CHUNK)
        rate = growth_b[part, :] * wind - damp_b[part, :] * loss
        send_rows[part, :] = (bent[part, :] * jnp.exp(rate)).astype(bf16)
        return carry

    lax.fori_loop(0, NCOMP // CHUNK, source, 0)

    pl.semaphore_wait(barrier, PEERS - 1 + 2)

    def give(other):
        pltpu.make_async_remote_copy(
            src_ref=send.at[other],
            dst_ref=recv.at[mz * GROUP + mq],
            send_sem=send_sem,
            recv_sem=recv_sem.at[mz],
            device_id={"comp": other},
            device_id_type=MESH,
        ).start()

    for_peers(give)
    own = pltpu.make_async_copy(send.at[me], recv.at[mz * GROUP + mq], own_sem)
    own.start()

    live_count = count_v[...]
    lane = lax.broadcasted_iota(jnp.int32, (1, BLOCK), 1)
    col_of = lax.broadcasted_iota(jnp.int16, (HALF, BLOCK), 0)
    row_of = 2 * lax.broadcasted_iota(jnp.int16, (ROWS, GROUP * BLOCK), 0)

    def factors(z, total):
        for q in range(GROUP):
            first = ((q // NCORE) * (NZ * NCORE) + z * NCORE + q % NCORE) * BLOCK
            cell = cells_v[:, pl.ds(pl.multiple_of(first, BLOCK), BLOCK)]
            col = jnp.broadcast_to(lax.bitwise_and(cell, HALF - 1), (HALF, BLOCK)).astype(jnp.int16)
            cols[z, :, q * BLOCK : (q + 1) * BLOCK] = jnp.where(col_of == col, bf16(1), bf16(0))
            row = jnp.where(lane + first < live_count, lax.shift_right_logical(cell, 8), 2 * ROWS)
            rowid[z, :, q * BLOCK : (q + 1) * BLOCK] = jnp.broadcast_to(row, (ROWS, BLOCK)).astype(jnp.int16)
        ids = rowid[z]
        hot = jnp.concatenate([jnp.where(ids == row_of + half, bf16(1), bf16(0)) for half in range(2)], axis=0)
        return total + lax.dot_general(hot, cols[z], (((1,), (1,)), ((), ())), preferred_element_type=f32)

    mask = lax.fori_loop(0, NZ, factors, jnp.zeros((2 * ROWS, HALF), f32))
    mask = jnp.concatenate([mask[:ROWS], mask[ROWS:]], axis=1)
    mask_bf[...] = mask.astype(bf16)
    mask_copies = []
    for i, other in enumerate((upper, lower)):
        copy = pltpu.make_async_remote_copy(
            src_ref=mask_bf,
            dst_ref=mask_in.at[i],
            send_sem=mask_send.at[i],
            recv_sem=mask_recv.at[i],
            device_id={"lat": other},
            device_id_type=MESH,
        )
        copy.start()
        mask_copies.append(copy)

    field[...] = jnp.zeros_like(field)
    tail[...] = jnp.zeros_like(tail)
    tail_d[...] = jnp.zeros_like(tail_d)
    speed = cour_s[me // 2]
    wx = face_weights(speed * table_v[0])
    wy = face_weights(speed * table_v[1])

    def wide(x, first, count):
        return jnp.concatenate([x[first : first + count]] * (LON // 128), axis=1)

    main_y = [wide(w, 0, MAIN) for w in wy]
    turned_x = [w[24:][None] for w in wx]
    tail_x, tail_y = [[x[MAIN:24][None] for x in w] for w in (wx, wy)]

    for copy in mask_copies:
        copy.wait()
    has_lower = jnp.where(lat > 0, 1.0, 0.0)
    has_upper = jnp.where(lat < TILES - 1, 1.0, 0.0)
    below = mask_in[0].astype(f32)[ROWS - 4 :] * has_lower
    above = mask_in[1].astype(f32)[:4] * has_upper
    full = jnp.concatenate([below, mask, above], axis=0)
    mask_x[...] = full
    open_x[...] = full * pltpu.roll(full, LON - 1, 1)
    open_y[...] = full * pltpu.roll(full, EXT - 1, 0)
    for wide_m, dense in ((mask_x, dense_m), (open_x, dense_x), (open_y, dense_y)):
        for t in range(EXT // 8):
            for b in range(LON // 128):
                piece = wide_m[t * 8 : (t + 1) * 8, b * 128 : (b + 1) * 128]
                for p in range(2):
                    dense[pl.ds(t * 64 + b * 2 + p, 8, stride=8), :] = piece

    for g, runs in enumerate(GROUPS):
        for b in range(LON // 128):
            lines = [
                jnp.broadcast_to(open_x[e : e + 1, b * 128 : (b + 1) * 128], (MAIN, 128)) for run in runs for e in run
            ]
            turned_open[g, b * 128 : (b + 1) * 128, :] = jnp.concatenate(lines, axis=0).T

    recv_rows = recv.reshape(PEERS * MINE, BLOCK)

    edge_rows = (0, 1, 2, 3, ROWS - 4, ROWS - 3, ROWS - 2, ROWS - 1)
    inner_rows = tuple(range(4, ROWS - 4))

    def left_factor(z, rows, with_tail):
        ids = rowid[z]
        starts = [(z * GROUP + q) * MINE for q in range(GROUP)]
        main = jnp.concatenate([recv_rows[pl.ds(first, MAIN), :] for first in starts], axis=1)
        parts = [jnp.where(ids == 2 * r + half, main, bf16(0)) for r in rows for half in range(2)]
        if with_tail:
            rest = jnp.concatenate([recv_rows[pl.ds(first + MAIN, 2), :] for first in starts], axis=1)
            for p in range(2):
                line = jnp.broadcast_to(rest[p : p + 1], (ROWS, GROUP * BLOCK))
                parts += [jnp.where(ids == row_of + half, line, bf16(0)) for half in range(2)]
        return jnp.concatenate(parts, axis=0)

    def place(zs, rows, with_tail):
        left = jnp.concatenate([left_factor(z, rows, with_tail) for z in zs], axis=1)
        right = jnp.concatenate([cols[z] for z in zs], axis=1)
        found = lax.dot_general(left, right, (((1,), (1,)), ((), ())), preferred_element_type=f32)
        for i, r in enumerate(rows):
            for half in range(2):
                field[4 + r, :, half * HALF : (half + 1) * HALF] += found[(2 * i + half) * MAIN : (2 * i + half + 1) * MAIN]
        if with_tail:
            first = 2 * len(rows) * MAIN
            for half in range(2):
                for p in range(2):
                    start = first + (2 * p + half) * ROWS
                    tail[p * ROWS : (p + 1) * ROWS, half * HALF : (half + 1) * HALF] += found[start : start + ROWS]

    def arrive(z, count):
        block = recv.at[pl.ds(z * GROUP, count)]
        pltpu.make_async_copy(block, block, recv_sem.at[z]).wait()

    def z_of(k):
        return jnp.where(k < NZ // 2, k, NZ + NZ // 2 - 1 - k)

    def place_edges(i, carry):
        zs = [z_of(i * BATCH + k) for k in range(BATCH)]

        for z in zs:
            pl.when(z != mz)(lambda z=z: arrive(z, GROUP))
        place(zs, edge_rows, True)
        return carry

    def place_inner(i, carry):
        place([i * BATCH + k for k in range(BATCH)], inner_rows, False)
        return carry

    own.wait()
    arrive(mz, GROUP - 1)
    lax.fori_loop(0, NZ // BATCH, place_edges, 0)

    forward = lax.rem(me, 2) == 0
    downstream = jnp.where(forward, upper, lower)
    upstream = jnp.where(forward, lower, upper)

    def tail_rows(p, r, b):
        return tail[p * ROWS + r : p * ROWS + r + 2, b * 128 : (b + 1) * 128]

    def pack(i, r, r_back):
        edge_out[i, :, :] = field[pl.ds(4 + (r if r == r_back else jnp.where(forward, r, r_back)), 2)].reshape(2 * MAIN, LON).astype(bf16)
        pieces = [jnp.where(forward, tail_rows(p, r, b), tail_rows(p, r_back, b)) for b in range(LON // 128) for p in range(2)]
        tail_out[i, :, :] = jnp.concatenate(pieces, axis=0).astype(bf16)

    def pack_first(r):
        pieces = [field[e, 0:1, b * 128 : (b + 1) * 128] for b in range(LON // 128) for e in (4 + r, 5 + r)]
        tail_out[3, :, :] = jnp.concatenate(pieces + [jnp.zeros((8, 128), f32)], axis=0).astype(bf16)

    edge_copies = []

    def swap(i, other):
        for j, (src, dst) in enumerate(((edge_out, edge_in), (tail_out, tail_in))):
            if i == 3 and j == 0:
                continue
            copy = pltpu.make_async_remote_copy(
                src_ref=src.at[i],
                dst_ref=dst.at[i],
                send_sem=edge_send.at[i, j],
                recv_sem=edge_recv.at[i, j],
                device_id={"lat": other},
                device_id_type=MESH,
            )
            copy.start()
            edge_copies.append(copy)

    pack(2, ROWS - 4, 2)
    swap(2, downstream)
    pack(0, ROWS - 2, ROWS - 2)
    swap(0, upper)
    pack(1, 0, 0)
    swap(1, lower)
    pack_first(jnp.where(forward, 2, ROWS - 4))
    swap(3, upstream)

    lax.fori_loop(0, NZ // BATCH, place_inner, 0)

    for p in range(2):
        for b in range(LON // 128):
            for t in range(2):
                tail_d[pl.ds(32 + t * 64 + b * 2 + p, 8, stride=8), :] = tail[
                    p * ROWS + t * 8 : p * ROWS + t * 8 + 8, b * 128 : (b + 1) * 128
                ]

    def change_x(src, rows, g):
        blocks = []
        for b in range(LON // 128):
            blocks.append(jnp.concatenate([src[e, :, b * 128 : (b + 1) * 128] for e in rows], axis=0).T)
        now = jnp.concatenate(blocks, axis=0)

        def tiles(x):
            return x.reshape(LON // 8, 8, 128)

        ahead, far, here, there = turned_x
        side = jnp.where(ahead, tiles(pltpu.roll(now, 1, 0)), tiles(pltpu.roll(now, LON - 2, 0)))
        east = far * side + here * tiles(now) + there * tiles(pltpu.roll(now, LON - 1, 0))
        east = (east * tiles(turned_open[g])).reshape(LON, 128)
        change = east - pltpu.roll(east, 1, 0)
        back = [change[b * 128 : (b + 1) * 128].T for b in range(LON // 128)]
        return {e: jnp.concatenate([x[i * MAIN : (i + 1) * MAIN] for x in back], axis=1) for i, e in enumerate(rows)}

    def advance(src, runs, store):
        moved = change_x(src, [e for run in runs for e in run], GROUPS.index(runs))
        ahead, far, here, there = main_y

        def flux_y(e):
            side = jnp.where(ahead, src[e - 1], src[e + 2])
            return (far * side + here * src[e] + there * src[e + 1]) * open_y[e : e + 1, :]

        for run in runs:
            south = flux_y(run[0] - 1)
            for e in run:
                north = flux_y(e)
                store(e, (src[e] - moved[e] - (north - south)) * mask_x[e : e + 1, :])
                south = north

    def keep(e, new):
        mid[e] = new

    def finish(e, new):
        for h in range(MAIN // 8):
            for b in range(LON // 128):
                out_v[b, pl.ds(h * 8 * ROWS + e - 4, 8, stride=ROWS), :] = new[h * 8 : h * 8 + 8, b * 128 : (b + 1) * 128]

    lane3 = lax.broadcasted_iota(jnp.int32, (1, 8, 128), 2)

    def west_of(x):
        turned = pltpu.roll(x, 1, 2)
        return jnp.where(lane3 == 0, pltpu.roll(turned, 2, 1), turned)

    def east_of(x, n):
        turned = pltpu.roll(x, 128 - n, 2)
        return jnp.where(lane3 >= 128 - n, pltpu.roll(turned, 6, 1), turned)

    def rows3(ref, start, count):
        return ref[start * 8 : (start + count) * 8, :].reshape(count, 8, 128)

    def advance_tail(full, first):
        count = full.shape[0] - 4
        now = full[2 : count + 2]
        ahead, far, here, there = tail_x
        side = jnp.where(ahead, west_of(now), east_of(now, 2))
        east = (far * side + here * now + there * east_of(now, 1)) * rows3(dense_x, first + 2, count)
        ahead, far, here, there = tail_y
        side = jnp.where(ahead, full[0 : count + 1], full[3 : count + 4])
        north = (far * side + here * full[1 : count + 2] + there * full[2 : count + 3]) * rows3(
            dense_y, first + 1, count + 1
        )
        return (now - (east - west_of(east)) - (north[1:] - north[:-1])) * rows3(dense_m, first + 2, count)

    for runs in FIRST_INNER:
        advance(field, runs, keep)
    for runs in SECOND_INNER:
        advance(mid, runs, finish)
    tail_half = advance_tail(rows3(tail_d, 4, ROWS), 4)
    tail_mid[48:144, :] = tail_half.reshape(96, 128)
    tail_done[32:96, :] = advance_tail(tail_half, 6).reshape(64, 128)

    for copy in edge_copies:
        copy.wait()
    def unpack(i, e, there):
        field[e : e + 2] = (edge_in[i].astype(f32) * there).reshape(2, MAIN, LON)
        ghost = tail_in[i].astype(f32) * there
        for k in range(8):
            tail_d[pl.ds(e * 8 + k, 2, stride=8), :] = ghost[2 * k : 2 * k + 2]

    unpack(0, 2, has_lower)
    unpack(1, EXT - 4, has_upper)

    def unpack_first(e, there):
        ghost = tail_in[3].astype(f32) * there
        for b in range(LON // 128):
            for i in range(2):
                field[e + i, 0:1, b * 128 : (b + 1) * 128] = ghost[2 * b + i : 2 * b + i + 1]

    @pl.when(forward)
    def _():
        unpack(2, 0, has_lower)
        unpack_first(EXT - 2, has_upper)

    @pl.when(jnp.logical_not(forward))
    def _():
        unpack(2, EXT - 2, has_upper)
        unpack_first(0, has_lower)

    for runs in FIRST_OUTER:
        advance(field, runs, keep)
    for runs in SECOND_OUTER:
        advance(mid, runs, finish)
    low = jnp.concatenate([advance_tail(rows3(tail_d, 0, 8), 0), rows3(tail_mid, 6, 4)], axis=0)
    tail_done[0:32, :] = advance_tail(low, 2).reshape(32, 128)
    high = jnp.concatenate([rows3(tail_mid, 14, 4), advance_tail(rows3(tail_d, 16, 8), 16)], axis=0)
    tail_done[96:128, :] = advance_tail(high, 14).reshape(32, 128)

    for b in range(LON // 128):
        out[: MAIN * ROWS, b * 128 : (b + 1) * 128] = out_v[b]
        for p in range(2):
            out[(MAIN + p) * ROWS : (MAIN + p + 1) * ROWS, b * 128 : (b + 1) * 128] = tail_done[
                pl.ds(b * 2 + p, ROWS, stride=8), :
            ]
    sent = send.at[pl.ds(0, PEERS - 1)]
    pltpu.make_async_copy(sent, sent, send_sem).wait()


def body(spectrum, sea_cells, sea_count, refraction, wind_speed, growth, damping, courant):
    vmem, smem, dma = pltpu.VMEM, pltpu.SMEM, pltpu.SemaphoreType.DMA
    table = jnp.asarray(direction_table())
    block = (PEERS, MINE // 2, 2, BLOCK)
    scratch = [
        vmem((NCOMP, BLOCK), bf16),
        vmem((1, SLOTS), jnp.int32),
        vmem((1, BLOCK), jnp.int32),
        vmem((1, BLOCK), f32),
        vmem((1, BLOCK), f32),
        vmem((NCOMP,), f32),
        vmem((NCOMP,), f32),
        smem((32,), f32),
        vmem((2, 32, 128), f32),
        vmem((NCOMP, BLOCK), f32),
        vmem((NCOMP, BLOCK), f32),
        vmem((NCOMP, BLOCK), f32),
        vmem(block, bf16),
        vmem(block, bf16),
        vmem((NZ, HALF, GROUP * BLOCK), bf16),
        vmem((NZ, ROWS, GROUP * BLOCK), jnp.int16),
        vmem((ROWS, LON), bf16),
        vmem((2, ROWS, LON), bf16),
        vmem((EXT, LON), f32),
        vmem((EXT, LON), f32),
        vmem((EXT, LON), f32),
        vmem((len(GROUPS), LON, 128), f32),
        vmem((EXT * 8, 128), f32),
        vmem((EXT * 8, 128), f32),
        vmem((EXT * 8, 128), f32),
        vmem((EXT, MAIN, LON), f32),
        vmem((EXT, MAIN, LON), f32),
        vmem((2 * ROWS, LON), f32),
        vmem((EXT * 8, 128), f32),
        vmem((EXT * 8, 128), f32),
        vmem((ROWS * 8, 128), f32),
        vmem((3, 2 * MAIN, LON), bf16),
        vmem((3, 2 * MAIN, LON), bf16),
        vmem((4, 16, 128), bf16),
        vmem((4, 16, 128), bf16),
        vmem((LON // 128, MAIN * ROWS, 128), f32),
        dma((9,)),
        dma,
        dma((NZ,)),
        dma,
        dma((2,)),
        dma((2,)),
        dma((4, 2)),
        dma((4, 2)),
    ]
    counts = jnp.broadcast_to(sea_count[None, :], (1, BLOCK))
    inputs = (spectrum, sea_cells, counts, refraction, wind_speed, growth, damping, courant, table)
    out = pl.pallas_call(
        kernel,
        out_shape=jax.ShapeDtypeStruct((MINE * ROWS, LON), f32),
        in_specs=[pl.BlockSpec(memory_space=pltpu.HBM)] * len(inputs),
        out_specs=pl.BlockSpec(memory_space=pltpu.VMEM),
        scratch_shapes=scratch,
        compiler_params=pltpu.CompilerParams(collective_id=0, has_side_effects=True, vmem_limit_bytes=40 << 20),
        name="wave_step",
    )(*[pltpu.with_memory_space_constraint(x, pltpu.HBM) for x in inputs])
    return out.reshape(MINE, ROWS, LON)


def solution(mesh):
    return jax.shard_map(
        body,
        mesh=mesh,
        in_specs=(
            P(None, ("lat", "comp")),
            P("lat", None),
            P("lat"),
            P("lat", None),
            P("lat", None),
            P(),
            P(),
            P(),
        ),
        out_specs=P("comp", "lat", None),
        check_vma=False,
    )
```
